32 devices in a mesh: seq: 8 (over z, y), fsdp: 4 (over x, core).
Axes of the slice: x: 2, y: 2, z: 4, core: 2. Of those that a mesh axis runs over, the one named last changes fastest.
Arguments:
- incoming_symbols: bfloat16 [4, 2048, 1024], P('fsdp', 'seq'), may hold values from -6 to 6
- downstream_slope: bfloat16 [4, 2048, 1024], P('fsdp', 'seq'), may hold values from -6 to 6
- sequence_extents: int32 [4, 8], P('fsdp'), may hold values from 0 to 2046, as said below
- mixer_lookup_map: bfloat16 [1024, 1024], P('fsdp'), may hold values from -0.1875 to 0.1875
- mixer_payload_map: bfloat16 [1024, 1024], P('fsdp'), may hold values from -0.1875 to 0.1875
- mixer_accepting_map: bfloat16 [1024, 1024], P('fsdp'), may hold values from -0.1875 to 0.1875
- mixer_emitted_map: bfloat16 [1024, 1024], P('fsdp'), may hold values from -0.375 to 0.375
- feedforward_lookup_map: bfloat16 [1024, 4096], P('fsdp'), may hold values from -0.1875 to 0.1875
- feedforward_payload_map: bfloat16 [4096, 1024], P('fsdp'), may hold values from -0.09375 to 0.09375
- feedforward_accepting_map: bfloat16 [1024, 1024], P('fsdp'), may hold values from -0.1875 to 0.1875
- prime_normalize_gain: float32 [1024], replicated, may hold values from 0.5 to 1.5
- prime_normalize_bias: float32 [1024], replicated, may hold values from -1.5 to 1.5
- later_normalize_gain: float32 [1024], replicated, may hold values from 0.5 to 1.5
- later_normalize_bias: float32 [1024], replicated, may hold values from -1.5 to 1.5
- mixer_lookup_shiftmix: float32 [1024], replicated, may hold values from 0.1 to 0.9
- mixer_payload_shiftmix: float32 [1024], replicated, may hold values from 0.1 to 0.9
- mixer_accepting_shiftmix: float32 [1024], replicated, may hold values from 0.1 to 0.9
- feedforward_lookup_shiftmix: float32 [1024], replicated, may hold values from 0.1 to 0.9
- feedforward_accepting_shiftmix: float32 [1024], replicated, may hold values from 0.1 to 0.9
- channel_shrink_rate: float32 [1024], replicated, may hold values from -7 to -3
- newest_boost: float32 [1024], replicated, may hold values from -1 to 1
Outputs:
- mixed: bfloat16 [4, 2048, 1024], P('fsdp', 'seq')
- tokens_grad: bfloat16 [4, 2048, 1024], P('fsdp', 'seq')
- att_key_grad: float32 [1024, 1024], P(('seq', 'fsdp'))
- att_value_grad: float32 [1024, 1024], P(('seq', 'fsdp'))
- att_recept_grad: float32 [1024, 1024], P(('seq', 'fsdp'))
- att_output_grad: float32 [1024, 1024], P(('seq', 'fsdp'))
- ffn_key_grad: float32 [1024, 4096], P(('seq', 'fsdp'))
- ffn_value_grad: float32 [4096, 1024], P(('seq', 'fsdp'))
- ffn_recept_grad: float32 [1024, 1024], P(('seq', 'fsdp'))
- first_gain_grad: float32 [1024], P(('seq', 'fsdp'))
- first_bias_grad: float32 [1024], P(('seq', 'fsdp'))
- derivative_post_scale_amplitude: float32 [1024], P(('seq', 'fsdp'))
- second_bias_grad: float32 [1024], P(('seq', 'fsdp'))
- mix_key_grad: float32 [1024], P(('seq', 'fsdp'))
- mix_value_grad: float32 [1024], P(('seq', 'fsdp'))
- mix_recept_grad: float32 [1024], P(('seq', 'fsdp'))
- ffn_mix_key_grad: float32 [1024], P(('seq', 'fsdp'))
- ffn_mix_recept_grad: float32 [1024], P(('seq', 'fsdp'))
- time_decay_grad: float32 [1024], P(('seq', 'fsdp'))
- time_first_grad: float32 [1024], P(('seq', 'fsdp'))
The draws below stay inside these ranges and needn't reach their ends.
Inputs may be any that keep to these rules, and one draw needn't show every extreme that they name: `sequence_extents`: row g lists three positive sequence lengths summing to 2048, then zeros; two of them are under 256 / 2. In some group both of these are 1.
All inputs are finite; a program needn't handle non-finite values.
Results may differ from the reference program's by a relative error of at most 0.02.
Values may be sent and summed in bfloat16 or wider, within the bound.
No kernel may reach another device: no remote copies, remote signals or barrier semaphores. Data moves between devices by JAX's collectives and lax.ppermute only.
A program may use at most 256 MiB of HBM per device.

```python
import jax
import jax.numpy as jnp
from jax import lax

FEATURE_COUNT = 1024
FF = 4096
TOK_DEV = 256
SLOTS = 8
GROUP_TOK = 2048
N_FSDP = 4


def draw_sequence_extents(key, part):
    key = jax.random.fold_in(key, 11)
    firsts = jax.random.randint(jax.random.fold_in(key, 1), (N_FSDP,), 1, TOK_DEV // 2)
    seconds = jax.random.randint(jax.random.fold_in(key, 2), (N_FSDP,), 1, TOK_DEV // 2)
    turns = jax.random.randint(jax.random.fold_in(key, 3), (N_FSDP,), 0, 3)
    chosen = jax.random.randint(jax.random.fold_in(key, 4), (), 0, N_FSDP)
    picked = jnp.arange(N_FSDP, dtype=jnp.int32) == chosen
    firsts = jnp.where(picked, 1, firsts)
    seconds = jnp.where(picked, 1, seconds)
    longest = GROUP_TOK - firsts - seconds
    trio = jnp.stack([firsts, seconds, longest], axis=1)
    places = (jnp.arange(3, dtype=jnp.int32)[None, :] + turns[:, None]) % 3
    trio = jnp.take_along_axis(trio, places, axis=1)
    padding = jnp.zeros((N_FSDP, SLOTS - 3), jnp.int32)
    return jnp.concatenate([trio, padding], axis=1).astype(jnp.int32)


def levels(rng, dims, cuts, least, largest):
    def one(position, shards_of):
        draws = jax.random.uniform(jax.random.fold_in(jax.random.fold_in(rng, 6), position), (shards_of,), jnp.float32, least / len(cuts), largest / len(cuts))
        return jnp.repeat(jnp.exp(draws), dims[position] // shards_of).reshape((-1,) + (1,) * (len(dims) - position - 1))

    gain = one(*cuts[0])
    for cut in cuts[1:]:
        gain = gain * one(*cut)
    return gain


def gaussian(key, extent, deviation, limit, pieces=(), kind=jnp.bfloat16):
    entries = jax.random.normal(key, extent, jnp.float32) * deviation
    if len(pieces) > 0:
        entries = levels(key, extent, pieces, -0.22, 0.18) * entries
    return jnp.clip(entries, min=-limit, max=limit).astype(kind)


def setup_inputs(seed: int = 0) -> dict:
    seeds = jax.random.split(jax.random.key(seed), 22)
    return {
        "incoming_symbols": gaussian(seeds[0], (N_FSDP, GROUP_TOK, FEATURE_COUNT), 1.0, 6.0, ((0, 4), (1, 8))),
        "downstream_slope": gaussian(seeds[1], (N_FSDP, GROUP_TOK, FEATURE_COUNT), 1.0, 6.0, ((0, 4), (1, 8))),
        "sequence_extents": draw_sequence_extents(jax.random.fold_in(seeds[21], 71), 0),
        "mixer_lookup_map": gaussian(seeds[3], (FEATURE_COUNT, FEATURE_COUNT), FEATURE_COUNT ** -0.5, 0.1875, ((0, 4),)),
        "mixer_payload_map": gaussian(seeds[4], (FEATURE_COUNT, FEATURE_COUNT), FEATURE_COUNT ** -0.5, 0.1875, ((0, 4),)),
        "mixer_accepting_map": gaussian(seeds[5], (FEATURE_COUNT, FEATURE_COUNT), FEATURE_COUNT ** -0.5, 0.1875, ((0, 4),)),
        "mixer_emitted_map": gaussian(seeds[6], (FEATURE_COUNT, FEATURE_COUNT), (FEATURE_COUNT // 4) ** -0.5, 0.375, ((0, 4),)),
        "feedforward_lookup_map": gaussian(seeds[7], (FEATURE_COUNT, FF), FEATURE_COUNT ** -0.5, 0.1875, ((0, 4),)),
        "feedforward_payload_map": gaussian(seeds[8], (FF, FEATURE_COUNT), FF ** -0.5, 0.09375, ((0, 4),)),
        "feedforward_accepting_map": gaussian(seeds[9], (FEATURE_COUNT, FEATURE_COUNT), FEATURE_COUNT ** -0.5, 0.1875, ((0, 4),)),
        "prime_normalize_gain": jnp.clip(1.0 + 0.1 * jax.random.normal(seeds[10], (FEATURE_COUNT,), jnp.float32), 0.5, 1.5),
        "prime_normalize_bias": gaussian(seeds[11], (FEATURE_COUNT,), 0.3, 1.5, (), jnp.float32),
        "later_normalize_gain": jnp.clip(1.0 + 0.1 * jax.random.normal(seeds[12], (FEATURE_COUNT,), jnp.float32), 0.5, 1.5),
        "later_normalize_bias": gaussian(seeds[13], (FEATURE_COUNT,), 0.3, 1.5, (), jnp.float32),
        "mixer_lookup_shiftmix": jnp.clip(jax.random.uniform(seeds[14], (FEATURE_COUNT,), jnp.float32, 0.1, 0.9), 0.1, 0.9),
        "mixer_payload_shiftmix": jnp.clip(jax.random.uniform(seeds[15], (FEATURE_COUNT,), jnp.float32, 0.1, 0.9), 0.1, 0.9),
        "mixer_accepting_shiftmix": jnp.clip(jax.random.uniform(seeds[16], (FEATURE_COUNT,), jnp.float32, 0.1, 0.9), 0.1, 0.9),
        "feedforward_lookup_shiftmix": jnp.clip(jax.random.uniform(seeds[17], (FEATURE_COUNT,), jnp.float32, 0.1, 0.9), 0.1, 0.9),
        "feedforward_accepting_shiftmix": jnp.clip(jax.random.uniform(seeds[18], (FEATURE_COUNT,), jnp.float32, 0.1, 0.9), 0.1, 0.9),
        "channel_shrink_rate": jnp.clip(jax.random.uniform(seeds[19], (FEATURE_COUNT,), jnp.float32, -7.0, -3.0), -7.0, -3.0),
        "newest_boost": jnp.clip(jax.random.uniform(seeds[20], (FEATURE_COUNT,), jnp.float32, -1.0, 1.0), -1.0, 1.0),
    }


norm_eps = 1e-05

@jax.custom_vjp
def low(v):
    return lax.optimization_barrier(v.astype(jnp.bfloat16)).astype(jnp.float32)

@jax.custom_vjp
def low_back(v):
    return v

def low_keep(v):
    return (low(v), None)

def low_pass(kept, grad):
    return (grad,)

def back_keep(v):
    return (v, None)

def back_low(kept, grad):
    return (low(grad),)
low.defvjp(low_keep, low_pass)
low_back.defvjp(back_keep, back_low)

def matmul(left, right):
    return jnp.dot(left, right, precision=lax.Precision.HIGHEST)

def layer_norm(hidden_track, gain_vec, bias_vec):
    centred = hidden_track - lax.optimization_barrier(jnp.mean(hidden_track, axis=-1, keepdims=True))
    spread = lax.optimization_barrier(jnp.mean(centred * centred, axis=-1, keepdims=True))
    return centred * lax.rsqrt(spread + norm_eps) * gain_vec + bias_vec

def shift_mix(current, previous, indicator_records, weights):
    retain = 1.0 - indicator_records.astype(jnp.float32)[:, None]
    shifted = jnp.concatenate([previous, current[:-1]], axis=0) * retain
    return tuple((current * weight + shifted * (1.0 - weight) for weight in weights))

def token_starts(sequence_extents, positions):
    begins = jnp.cumsum(sequence_extents, axis=-1) - sequence_extents
    start_marks = (begins[..., :, None] == positions) & (sequence_extents[..., :, None] > 0)
    return jnp.any(start_marks, axis=-2)

def tier_advance(hidden_track, indicator_records, lookup_map, payload_map, accepting_map, emitted_map, expanding_map, contracting_map, sigmoid_switch_map, prime_normalize_gain, prime_normalize_bias, later_normalize_gain, later_normalize_bias, mixer_lookup_shiftmix, mixer_payload_shiftmix, mixer_accepting_shiftmix, feedforward_lookup_shiftmix, feedforward_accepting_shiftmix, channel_shrink_rate, newest_boost):
    model_width = hidden_track.shape[1]
    block_rows = min(4096, hidden_track.shape[0])
    block_count = hidden_track.shape[0] // block_rows
    decay_rate = jnp.exp(channel_shrink_rate)
    fading = jnp.exp(-decay_rate)
    additional_first_reinforcement = jnp.exp(newest_boost)

    def recurrence(state_pair, entry):
        upper_fraction_sum, lower_fraction_sum = state_pair
        key_row, payload_item, flag_value = entry
        retain = 1.0 - flag_value
        upper_fraction_sum = upper_fraction_sum * retain
        lower_fraction_sum = lower_fraction_sum * retain
        powered_couplings = jnp.exp(key_row)
        ultimate_produced = (upper_fraction_sum + additional_first_reinforcement * powered_couplings * payload_item) / (lower_fraction_sum + additional_first_reinforcement * powered_couplings)
        return ((fading * upper_fraction_sum + powered_couplings * payload_item, fading * lower_fraction_sum + powered_couplings), ultimate_produced)

    def one_block(running, entry):
        rows_in, block_flags = entry
        last_normed, last_second, upper_fraction_sum, lower_fraction_sum = running
        normed = layer_norm(rows_in, prime_normalize_gain, prime_normalize_bias)
        key_in, value_in, recept_in = shift_mix(normed, last_normed[None], block_flags, (mixer_lookup_shiftmix, mixer_payload_shiftmix, mixer_accepting_shiftmix))
        lookup_records = low_back(low(matmul(low(key_in), lookup_map)))
        payload_records = low_back(low(matmul(low(value_in), payload_map)))
        recept = jax.nn.sigmoid(low_back(matmul(low(recept_in), accepting_map)))
        (upper_fraction_sum, lower_fraction_sum), wkv_rows = lax.scan(recurrence, (upper_fraction_sum, lower_fraction_sum), (lookup_records, payload_records, block_flags.astype(jnp.float32)))
        wkv_rows = low_back(low(wkv_rows))
        attended = low(recept * wkv_rows)
        resid = rows_in + low_back(matmul(attended, emitted_map))
        second = layer_norm(resid, later_normalize_gain, later_normalize_bias)
        up_in, gate_in = shift_mix(second, last_second[None], block_flags, (feedforward_lookup_shiftmix, feedforward_accepting_shiftmix))
        pre_up = low_back(matmul(low(up_in), expanding_map))
        squared = low(jnp.square(jnp.maximum(pre_up, 0.0)))
        ffn_vals = low_back(matmul(squared, contracting_map))
        gating = jax.nn.sigmoid(low_back(matmul(low(gate_in), sigmoid_switch_map)))
        ultimate_produced = resid + gating * ffn_vals
        return ((normed[-1], second[-1], upper_fraction_sum, lower_fraction_sum), ultimate_produced)
    zero_row = jnp.zeros((model_width,), jnp.float32)
    blocks = (hidden_track.reshape(block_count, block_rows, model_width), indicator_records.reshape(block_count, block_rows))
    unused_state, outputs = lax.scan(jax.checkpoint(one_block), (zero_row, zero_row, zero_row, zero_row), blocks)
    return outputs.reshape(hidden_track.shape)

def reference(incoming_symbols, downstream_slope, sequence_extents, mixer_lookup_map, mixer_payload_map, mixer_accepting_map, mixer_emitted_map, feedforward_lookup_map, feedforward_payload_map, feedforward_accepting_map, prime_normalize_gain, prime_normalize_bias, later_normalize_gain, later_normalize_bias, mixer_lookup_shiftmix, mixer_payload_shiftmix, mixer_accepting_shiftmix, feedforward_lookup_shiftmix, feedforward_accepting_shiftmix, channel_shrink_rate, newest_boost):
    group_len = incoming_symbols.shape[1]
    positions = jnp.arange(group_len, dtype=jnp.int32)
    indicator_records = token_starts(sequence_extents, positions).reshape(-1)
    model_width = incoming_symbols.shape[2]
    hidden_track = incoming_symbols.astype(jnp.float32).reshape(-1, model_width)
    weights = tuple((matrix.astype(jnp.float32) for matrix in (mixer_lookup_map, mixer_payload_map, mixer_accepting_map, mixer_emitted_map, feedforward_lookup_map, feedforward_payload_map, feedforward_accepting_map)))
    feature_lists = (prime_normalize_gain, prime_normalize_bias, later_normalize_gain, later_normalize_bias, mixer_lookup_shiftmix, mixer_payload_shiftmix, mixer_accepting_shiftmix, feedforward_lookup_shiftmix, feedforward_accepting_shiftmix, channel_shrink_rate, newest_boost)

    def forward(stream_in, *params):
        return tier_advance(stream_in, indicator_records, *params)
    outputs, backward = jax.vjp(forward, hidden_track, *weights, *feature_lists)
    grads = backward(downstream_slope.astype(jnp.float32).reshape(-1, model_width))
    return (outputs.reshape(incoming_symbols.shape).astype(jnp.bfloat16), grads[0].reshape(incoming_symbols.shape).astype(jnp.bfloat16), grads[1], grads[2], grads[3], grads[4], grads[5], grads[6], grads[7], grads[8], grads[9], grads[10], grads[11], grads[12], grads[13], grads[14], grads[15], grads[16], grads[17], grads[18])
```

```python
from functools import partial

import jax
import jax.numpy as jnp
from jax import lax
from jax.experimental import pallas as pl
from jax.experimental.pallas import tpu as pltpu
from jax.sharding import PartitionSpec as P

norm_eps = 1e-05
F32 = jnp.float32
BF16 = jnp.bfloat16
FAR = 1 << 20
BOTH = ("seq", "fsdp")


def flipped(value, axis, bit):
    count = lax.axis_size(axis)
    return lax.ppermute(value, axis, [(i, i ^ (1 << bit)) for i in range(count)])


def passed_along(value, axis, steps):
    count = lax.axis_size(axis)
    initial, last = (max(0, -steps), min(count, count - steps))
    return lax.ppermute(value, axis, [(source, source + steps) for source in range(initial, last)])


def layer_norm(hidden_track, gain_vec, bias_vec):
    centred = hidden_track - jnp.mean(hidden_track, axis=-1, keepdims=True)
    spread = jnp.mean(centred * centred, axis=-1, keepdims=True)
    return centred * lax.rsqrt(spread + norm_eps) * gain_vec + bias_vec


def shift_mix(current, previous, indicator_records, weights):
    retain = 1.0 - indicator_records.astype(F32)[:, None]
    shifted = jnp.concatenate([previous, current[:-1]], axis=0) * retain
    return tuple((current * weight + shifted * (1.0 - weight) for weight in weights))


def token_starts(sequence_extents, positions):
    begins = jnp.cumsum(sequence_extents, axis=-1) - sequence_extents
    start_marks = (begins[..., :, None] == positions) & (sequence_extents[..., :, None] > 0)
    return jnp.any(start_marks, axis=-2)


def scan_forward_body(rate_ref, k_ref, v_ref, since_ref, a_ref, b_ref, end_ref):
    rows, cols = k_ref.shape
    place = lax.broadcasted_iota(jnp.int32, (8, cols), 0)
    rate = rate_ref[...]
    fades = [jnp.exp(-rate * float(d)) for d in (1, 2, 4)]
    carry_fade = jnp.exp(-rate * (place + 1).astype(F32))

    def sub(k, v, since, state):
        lift = jnp.exp(k)
        near = jnp.minimum(since, place)
        out = []
        for run, last in zip((lift * v, lift), state):
            for d, fade in zip((1, 2, 4), fades):
                run = run + jnp.where(near >= d, fade * pltpu.roll(run, d, 0), 0.0)
            run = run + jnp.where(since > place, carry_fade * last, 0.0)
            before = jnp.where(place == 0, last, pltpu.roll(run, 1, 0))
            before = jnp.where(since >= 1, before, 0.0)
            out.append((before, run[7:8, :]))
        return out

    def step(i, state):
        base = pl.multiple_of(i * 16, 16)
        k = k_ref[pl.ds(base, 16), :].astype(F32)
        v = v_ref[pl.ds(base, 16), :].astype(F32)
        for h in range(2):
            at = pl.multiple_of(base + 8 * h, 8)
            since = jnp.tile(since_ref[pl.ds(at, 8), :], (1, cols // 128))
            (ua, sa), (ub, sb) = sub(k[8 * h : 8 * h + 8], v[8 * h : 8 * h + 8], since, state)
            a_ref[pl.ds(at, 8), :] = ua
            b_ref[pl.ds(at, 8), :] = ub
            state = (sa, sb)
        return state

    zero = jnp.zeros((1, cols), F32)
    sa, sb = lax.fori_loop(0, rows // 16, step, (zero, zero))
    end_ref[...] = jnp.where(place == 0, sa, jnp.where(place == 1, sb, 0.0))


def scan_backward_body(
    rate_ref, bonus_ref, k_ref, v_ref, d_ref, a_in_ref, b_in_ref, until_ref, a_ref, b_ref, end_ref
):
    rows, cols = k_ref.shape
    place = lax.broadcasted_iota(jnp.int32, (8, cols), 0)
    rate = rate_ref[...]
    fades = [jnp.exp(-rate * float(d)) for d in (1, 2, 4)]
    carry_fade = jnp.exp(-rate * (8 - place).astype(F32))

    def step(j, state):
        i = rows // 16 - 1 - j
        base = pl.multiple_of(i * 16, 16)
        k = k_ref[pl.ds(base, 16), :].astype(F32)
        v = v_ref[pl.ds(base, 16), :].astype(F32)
        d = d_ref[pl.ds(base, 16), :].astype(F32)
        for h in (1, 0):
            at = pl.multiple_of(base + 8 * h, 8)
            part = slice(8 * h, 8 * h + 8)
            until = jnp.tile(until_ref[pl.ds(at, 8), :], (1, cols // 128))
            near = jnp.minimum(until, 7 - place)
            bonus = jnp.exp(bonus_ref[...] + k[part])
            inverse = 1.0 / (b_in_ref[pl.ds(at, 8), :] + bonus)
            wkv = (a_in_ref[pl.ds(at, 8), :] + bonus * v[part]) * inverse
            first = d[part] * inverse
            new = []
            for run, last, ref in zip((first, -first * wkv), state, (a_ref, b_ref)):
                for q, fade in zip((1, 2, 4), fades):
                    run = run + jnp.where(near >= q, fade * pltpu.roll(run, 8 - q, 0), 0.0)
                run = run + jnp.where(until >= 8 - place, carry_fade * last, 0.0)
                after = jnp.where(place == 7, last, pltpu.roll(run, 7, 0))
                ref[pl.ds(at, 8), :] = jnp.where(until >= 1, after, 0.0)
                new.append(run[0:1, :])
            state = tuple(new)
        return state

    zero = jnp.zeros((1, cols), F32)
    sa, sb = lax.fori_loop(0, rows // 16, step, (zero, zero))
    end_ref[...] = jnp.where(place == 0, sa, jnp.where(place == 1, sb, 0.0))


def scan_call(body, vectors, arrays, marks):
    rows, cols = arrays[0].shape
    wide = min(256, cols)
    vec = pl.BlockSpec((1, wide), lambda i: (0, i))
    arr = pl.BlockSpec((rows, wide), lambda i: (0, i))
    return pl.pallas_call(
        body,
        grid=(cols // wide,),
        in_specs=[vec] * len(vectors)
        + [arr] * len(arrays)
        + [pl.BlockSpec((rows, 128), lambda i: (0, 0))],
        out_specs=[arr, arr, pl.BlockSpec((8, wide), lambda i: (0, i))],
        out_shape=[
            jax.ShapeDtypeStruct((rows, cols), F32),
            jax.ShapeDtypeStruct((rows, cols), F32),
            jax.ShapeDtypeStruct((8, cols), F32),
        ],
        cost_estimate=pl.CostEstimate(
            flops=60 * rows * cols, bytes_accessed=16 * rows * cols, transcendentals=rows * cols
        ),
    )(*[v[None, :] for v in vectors], *arrays, marks)


def gathered_ends(ends):
    count = lax.axis_size("seq")
    copies = jnp.broadcast_to(ends[None], (count, *ends.shape))
    return lax.all_to_all(copies, "seq", split_axis=0, concat_axis=0, tiled=True)


def scattered_sum(grad, order, here):
    rows, cols = grad.shape
    seq_count, fsdp_count = lax.axis_size("seq"), lax.axis_size("fsdp")
    line = seq_count // 2
    block = rows // (seq_count * fsdp_count)
    value = grad.reshape(line, 2, 2, 2, block, cols)
    dims = ["z", "y", "x", "c"]
    links = {"y": ("seq", 0), "x": ("fsdp", 1), "c": ("fsdp", 0)}
    for name in order:
        dim = dims.index(name)
        dims.pop(dim)
        if name == "z":
            value = line_sum(value, dim, here["z"], line)
            continue
        axis, bit = links[name]
        away = lax.dynamic_index_in_dim(value, 1 - here[name], dim, keepdims=False)
        got = flipped(away.astype(BF16), axis, bit)
        mine = lax.dynamic_index_in_dim(value, here[name], dim, keepdims=False)
        value = mine.astype(F32) + got.astype(F32)
    return value


def line_sum(value, dim, place, line):
    if line > 4:
        groups = [[2 * i + y for i in range(line)] for y in range(2)]
        whole = jnp.moveaxis(value, dim, 0)
        return lax.psum_scatter(whole, "seq", scatter_dimension=0, axis_index_groups=groups)
    up = down = None
    for step in range(1, line):
        sent_up = lax.dynamic_index_in_dim(
            value, jnp.minimum(place + line - step, line - 1), dim, keepdims=False
        ).astype(F32)
        sent_down = lax.dynamic_index_in_dim(
            value, jnp.maximum(place - line + step, 0), dim, keepdims=False
        ).astype(F32)
        if up is not None:
            sent_up = sent_up + up.astype(F32)
            sent_down = sent_down + down.astype(F32)
        up = lax.ppermute(
            sent_up.astype(BF16),
            "seq",
            [(2 * z + y, 2 * z + 2 + y) for z in range(step) for y in range(2)],
        )
        down = lax.ppermute(
            sent_down.astype(BF16),
            "seq",
            [(2 * z + y, 2 * z - 2 + y) for z in range(line - step, line) for y in range(2)],
        )
    mine = lax.dynamic_index_in_dim(value, place, dim, keepdims=False)
    return mine.astype(F32) + up.astype(F32) + down.astype(F32)


def on_device(
    incoming_symbols,
    downstream_slope,
    sequence_extents,
    mixer_lookup_map,
    mixer_payload_map,
    mixer_accepting_map,
    mixer_emitted_map,
    feedforward_lookup_map,
    feedforward_payload_map,
    feedforward_accepting_map,
    prime_normalize_gain,
    prime_normalize_bias,
    later_normalize_gain,
    later_normalize_bias,
    mixer_lookup_shiftmix,
    mixer_payload_shiftmix,
    mixer_accepting_shiftmix,
    feedforward_lookup_shiftmix,
    feedforward_accepting_shiftmix,
    channel_shrink_rate,
    newest_boost,
):
    hidden_track = incoming_symbols[0].astype(F32)
    tok_count, model_width = hidden_track.shape
    seq_count, fsdp_count = lax.axis_size("seq"), lax.axis_size("fsdp")
    sequence_number, fsdp_number = lax.axis_index("seq"), lax.axis_index("fsdp")
    here = {
        "z": sequence_number // 2,
        "y": sequence_number % 2,
        "x": fsdp_number // 2,
        "c": fsdp_number % 2,
    }

    group_positions = jnp.arange(tok_count * seq_count, dtype=jnp.int32)
    group_flags = token_starts(sequence_extents[0], group_positions)
    chunk_flags = group_flags.reshape(seq_count, tok_count)
    local_flags = lax.dynamic_index_in_dim(chunk_flags, sequence_number, 0, keepdims=False)
    chunk_has = jnp.any(chunk_flags, axis=1)
    chunk_first = chunk_flags[:, 0]
    places = jnp.arange(tok_count, dtype=jnp.int32)
    later = places[None, :] > places[:, None]
    last_start = jnp.max(
        jnp.where(local_flags[None, :] & ~later, places[None, :], -FAR), axis=1
    )
    next_start = jnp.min(jnp.where(local_flags[None, :] & later, places[None, :], FAR), axis=1)
    since = places - last_start
    until = next_start - 1 - places
    since_wide = jnp.broadcast_to(since[:, None], (tok_count, 128))
    until_wide = jnp.broadcast_to(until[:, None], (tok_count, 128))

    def whole(weight):
        return lax.all_gather(weight, "fsdp", axis=0, tiled=True)

    lookup_map = whole(mixer_lookup_map)
    payload_map = whole(mixer_payload_map)
    accepting_map = whole(mixer_accepting_map)
    emitted_map = whole(mixer_emitted_map)
    sigmoid_switch_map = whole(feedforward_accepting_map)
    expanding_map = whole(feedforward_lookup_map)
    contracting_map = whole(feedforward_payload_map)

    normed, first_back = jax.vjp(
        layer_norm, hidden_track, prime_normalize_gain, prime_normalize_bias
    )
    prior_row = passed_along(normed[-1:], "seq", 1)

    def mix(current, previous, weights):
        return shift_mix(current, previous, local_flags, weights)

    (key_in, value_in, recept_in), mix_one_back = jax.vjp(
        mix,
        normed,
        prior_row,
        (mixer_lookup_shiftmix, mixer_payload_shiftmix, mixer_accepting_shiftmix),
    )
    key_low = key_in.astype(BF16)
    value_low = value_in.astype(BF16)
    recept_low = recept_in.astype(BF16)
    key_rows = jnp.dot(key_low, lookup_map, preferred_element_type=F32).astype(BF16)
    value_rows = jnp.dot(value_low, payload_map, preferred_element_type=F32).astype(BF16)
    rate = jnp.exp(channel_shrink_rate)
    part_a, part_b, ends = scan_call(
        scan_forward_body, (rate,), (key_rows, value_rows), since_wide
    )
    all_ends = gathered_ends(ends[:2])
    recept = jax.nn.sigmoid(jnp.dot(recept_low, accepting_map, preferred_element_type=F32))
    order = jnp.arange(seq_count, dtype=jnp.int32)
    between = (order[None, :] > order[:, None]) & (order[None, :] < sequence_number)
    reaches = (order < sequence_number) & ~jnp.any(between & chunk_has[None, :], axis=1)
    gap = ((sequence_number - 1 - order) * tok_count).astype(F32)
    weigh = jnp.where(reaches[:, None], jnp.exp(-rate[None, :] * gap[:, None]), 0.0)
    entering = jnp.sum(weigh[:, None, :] * all_ends, axis=0)
    into = jnp.where(
        (since > places)[:, None], jnp.exp(-rate[None, :] * places.astype(F32)[:, None]), 0.0
    )
    key_float, value_float = key_rows.astype(F32), value_rows.astype(F32)
    state_a = part_a + into * entering[0:1]
    state_b = part_b + into * entering[1:2]
    bonus = jnp.exp(newest_boost + key_float)
    divisor = state_b + bonus
    wkv = (state_a + bonus * value_float) / divisor
    wkv_float = wkv.astype(BF16).astype(F32)
    attended = (recept * wkv_float).astype(BF16)
    resid = hidden_track + jnp.dot(attended, emitted_map, preferred_element_type=F32)

    second, second_back = jax.vjp(layer_norm, resid, later_normalize_gain, later_normalize_bias)
    prior_second = passed_along(second[-1:], "seq", 1)
    (up_in, gate_in), mix_two_back = jax.vjp(
        mix,
        second,
        prior_second,
        (feedforward_lookup_shiftmix, feedforward_accepting_shiftmix),
    )
    up_low = up_in.astype(BF16)
    gate_low = gate_in.astype(BF16)
    gating = jax.nn.sigmoid(jnp.dot(gate_low, sigmoid_switch_map, preferred_element_type=F32))
    pre_up = jnp.dot(up_low, expanding_map, preferred_element_type=F32)
    positive = jnp.maximum(pre_up, 0.0)
    squared = (positive * positive).astype(BF16)
    ffn_vals = jnp.dot(squared, contracting_map, preferred_element_type=F32)
    mixed = (resid + gating * ffn_vals).astype(BF16)

    upstream = downstream_slope[0].astype(F32)
    d_vals = (upstream * gating).astype(BF16)
    d_gate_pre = (upstream * ffn_vals * gating * (1.0 - gating)).astype(BF16)
    d_squared = jnp.dot(d_vals, contracting_map.T, preferred_element_type=F32)
    d_pre_up = (d_squared * 2.0 * positive).astype(BF16)
    grad_down = scattered_sum(
        jnp.dot(squared.T, d_vals, preferred_element_type=F32), "cxyz", here
    )
    d_up_in = jnp.dot(d_pre_up, expanding_map.T, preferred_element_type=F32)
    d_gate_in = jnp.dot(d_gate_pre, sigmoid_switch_map.T, preferred_element_type=F32)
    grad_up = scattered_sum(jnp.dot(up_low.T, d_pre_up, preferred_element_type=F32), "cyxz", here)
    grad_gate = scattered_sum(
        jnp.dot(gate_low.T, d_gate_pre, preferred_element_type=F32), "czxy", here
    )
    d_second, d_prior_second, (grad_ffn_mix_key, grad_ffn_mix_recept) = mix_two_back(
        (d_up_in, d_gate_in)
    )
    returned_second = passed_along(d_prior_second, "seq", -1)
    d_second = jnp.concatenate([d_second[:-1], d_second[-1:] + returned_second], axis=0)
    d_resid_norm, grad_second_gain, grad_second_bias = second_back(d_second)
    d_resid = upstream + d_resid_norm

    d_att = d_resid.astype(BF16)
    d_attended = jnp.dot(d_att, emitted_map.T, preferred_element_type=F32)
    d_wkv_low = (d_attended * recept).astype(BF16)
    d_recept_pre = (d_attended * wkv_float * recept * (1.0 - recept)).astype(BF16)
    back_a, back_b, heads = scan_call(
        scan_backward_body,
        (rate, newest_boost),
        (key_rows, value_rows, d_wkv_low, state_a, state_b),
        until_wide,
    )
    all_heads = gathered_ends(heads[:2])
    grad_output = scattered_sum(
        jnp.dot(attended.T, d_att, preferred_element_type=F32), "czyx", here
    )
    grad_recept = scattered_sum(
        jnp.dot(recept_low.T, d_recept_pre, preferred_element_type=F32), "czxy", here
    )
    d_recept_in = jnp.dot(d_recept_pre, accepting_map.T, preferred_element_type=F32)
    blocked = chunk_first[None, :] & (order[None, :] <= order[:, None])
    blocked = blocked & (order[None, :] > sequence_number)
    inner = chunk_has[None, :] & (order[None, :] > sequence_number)
    inner = inner & (order[None, :] < order[:, None])
    comes = (order > sequence_number) & ~jnp.any(blocked | inner, axis=1)
    gap_back = ((order - 1 - sequence_number) * tok_count).astype(F32)
    weigh_back = jnp.where(comes[:, None], jnp.exp(-rate[None, :] * gap_back[:, None]), 0.0)
    returning = jnp.sum(weigh_back[:, None, :] * all_heads, axis=0)
    rest = (tok_count - 1 - places).astype(F32)
    out_of = jnp.where(
        (until > tok_count)[:, None], jnp.exp(-rate[None, :] * rest[:, None]), 0.0
    )
    next_a = back_a + out_of * returning[0:1]
    next_b = back_b + out_of * returning[1:2]
    lift = jnp.exp(key_float)
    d_wkv = d_wkv_low.astype(F32)
    ratio = bonus * d_wkv / divisor
    gap_value = ratio * (value_float - wkv)
    d_key_low = (gap_value + lift * (value_float * next_a + next_b)).astype(BF16)
    d_value_low = (ratio + lift * next_a).astype(BF16)
    grad_first = jnp.sum(gap_value, axis=0)
    grad_decay = -rate * jnp.exp(-rate) * jnp.sum(next_a * state_a + next_b * state_b, axis=0)

    grad_key = scattered_sum(
        jnp.dot(key_low.T, d_key_low, preferred_element_type=F32), "cxyz", here
    )
    grad_value = scattered_sum(
        jnp.dot(value_low.T, d_value_low, preferred_element_type=F32), "cyxz", here
    )
    d_key_in = jnp.dot(d_key_low, lookup_map.T, preferred_element_type=F32)
    d_value_in = jnp.dot(d_value_low, payload_map.T, preferred_element_type=F32)
    d_normed, d_prior, (grad_mix_key, grad_mix_value, grad_mix_recept) = mix_one_back(
        (d_key_in, d_value_in, d_recept_in)
    )
    returned_first = passed_along(d_prior, "seq", -1)
    d_normed = jnp.concatenate([d_normed[:-1], d_normed[-1:] + returned_first], axis=0)
    d_stream_norm, grad_first_gain, grad_first_bias = first_back(d_normed)
    tokens_grad = (d_resid + d_stream_norm).astype(BF16)[None]

    small = jnp.stack(
        [
            grad_first_gain,
            grad_first_bias,
            grad_second_gain,
            grad_second_bias,
            grad_mix_key,
            grad_mix_value,
            grad_mix_recept,
            grad_ffn_mix_key,
            grad_ffn_mix_recept,
            grad_decay,
            grad_first,
        ]
    )
    owners = seq_count * fsdp_count
    share = model_width // owners
    small = small.reshape(-1, owners, share).transpose(1, 0, 2).reshape(owners, -1)
    small = lax.all_to_all(small, BOTH, split_axis=0, concat_axis=0, tiled=True)
    small = jnp.sum(small, axis=0).reshape(-1, share)
    large = (grad_key, grad_value, grad_recept, grad_output, grad_up, grad_down, grad_gate)
    return (mixed[None], tokens_grad, *large, *[small[i] for i in range(11)])


def solution(mesh):
    rows = P("fsdp", None)
    tokens = P("fsdp", "seq", None)
    return jax.shard_map(
        on_device,
        mesh=mesh,
        in_specs=(tokens, tokens, *[rows] * 8, *[P()] * 11),
        out_specs=(tokens, tokens, *[P(BOTH, None)] * 7, *[P(BOTH)] * 11),
        check_vma=False,
    )
```

```python
from functools import partial

import jax
import jax.numpy as jnp
from jax import lax
from jax.experimental import pallas as pl
from jax.experimental.pallas import tpu as pltpu
from jax.sharding import PartitionSpec as P

norm_eps = 1e-05
F32 = jnp.float32
BF16 = jnp.bfloat16
FAR = 1 << 20
SLIGHT = pl.CostEstimate(flops=1, bytes_accessed=1, transcendentals=0)
NEVER = 1e30
BOTH = ("seq", "fsdp")
LINKS = {"c": ("fsdp", 0), "x": ("fsdp", 1), "y": ("seq", 0), "z0": ("seq", 1)}
VMEM = pl.BlockSpec(memory_space=pltpu.VMEM)
SMEM = pl.BlockSpec(memory_space=pltpu.SMEM)
HBM = pl.BlockSpec(memory_space=pl.ANY)
WIDE = 512
STEP = 32


def after(value, *others):
    return lax.optimization_barrier((value, others))[0]


def flipped(value, axis, bit):
    count = lax.axis_size(axis)
    return lax.ppermute(value, axis, [(i, i ^ (1 << bit)) for i in range(count)])


def passed_along(value, axis, steps):
    count = lax.axis_size(axis)
    initial, last = (max(0, -steps), min(count, count - steps))
    return lax.ppermute(value, axis, [(source, source + steps) for source in range(initial, last)])


def token_starts(sequence_extents, positions):
    begins = jnp.cumsum(sequence_extents, axis=-1) - sequence_extents
    start_marks = (begins[..., :, None] == positions) & (sequence_extents[..., :, None] > 0)
    return jnp.any(start_marks, axis=-2)


def gathered_ends(ends):
    count = lax.axis_size("seq")
    copies = jnp.broadcast_to(ends[None], (count, *ends.shape))
    return lax.all_to_all(copies, "seq", split_axis=0, concat_axis=0, tiled=True)


def across(left, right):
    return lax.dot_general(left, right, (((1,), (1,)), ((), ())), preferred_element_type=F32)


def spread(mark, cols):
    return jnp.tile(mark, (1, cols // 128))


def normal(z):
    centred = z - jnp.mean(z, axis=-1, keepdims=True)
    return centred, lax.rsqrt(jnp.mean(centred * centred, axis=-1, keepdims=True) + norm_eps)


def normal_back(z, d, gain):
    centred, scale = normal(z)
    n = centred * scale
    e = d * gain
    inner = e - jnp.mean(e, axis=-1, keepdims=True) - n * jnp.mean(e * n, axis=-1, keepdims=True)
    return n, scale * inner


def one_later(block, previous):
    place = lax.broadcasted_iota(jnp.int32, block.shape, 0)
    return jnp.where(place == 0, previous, pltpu.roll(block, 1, 0))


def one_earlier(block, following):
    rows = block.shape[0]
    place = lax.broadcasted_iota(jnp.int32, block.shape, 0)
    return jnp.where(place == rows - 1, following, pltpu.roll(block, rows - 1, 0))


def folded(block):
    return sum(block[n : n + 8] for n in range(0, block.shape[0], 8))


def turn_blocks(index_ref, n, source, whole, away, mine):
    owners = index_ref.shape[1]
    block = source.shape[1] // owners
    whole[...] = source[...].T
    for r in range(owners):
        base = pl.multiple_of(index_ref[n, r] * block, block)
        out, at = (away, r) if r < owners // 2 else (mine, r - owners // 2)
        out[n, at * block : (at + 1) * block, :] = whole[pl.ds(base, block), :]


def turns_in_kernel(rows, streams):
    return (rows // streams[0].blocks.shape[0]) % 16 == 0


def turned_outside(acts, streams):
    rows = acts[0].shape[1]
    out = []
    for act, stream in zip(acts, streams):
        block = rows // stream.blocks.shape[0]
        index = stream.blocks[:, None] * block + jnp.arange(block)[None, :]
        out.append(jnp.take(act.T, index.reshape(-1), axis=0))
    out = jnp.stack(out)
    return out[:, : rows // 2], out[:, rows // 2 :]


class Piece:
    def __init__(self, part, offset, lead=(), rows=None, column=None):
        self.part, self.offset, self.lead = part, offset, lead
        self.rows, self.column = rows, column


def listed(plans):
    parts, offsets, copies = [], [], []
    for plan in plans:
        copies.append([])
        for piece in plan:
            known = [n for n, p in enumerate(parts) if p is piece.part]
            if not known:
                parts.append(piece.part)
                known = [len(parts) - 1]
            copies[-1].append((known[0], piece, len(offsets)))
            offsets.append(piece.offset)
    return parts, jnp.stack(offsets).astype(jnp.int32), copies


def copied(copies, ins, offset_ref, whole, sems, columns=None):
    started = []
    for n, (part, piece, which) in enumerate(copies):
        source = ins[part].at[piece.lead] if piece.lead else ins[part]
        if piece.rows is not None:
            source = source.at[piece.rows, :]
        base = pl.multiple_of(offset_ref[which], 16)
        target = pl.ds(base, source.shape[0])
        if piece.column is not None:
            taken = slice(piece.column, piece.column + source.shape[1])
            if columns is not None and taken.start != columns.start:
                continue
        elif columns is not None:
            taken = columns
            source = source.at[:, columns]
        else:
            taken = slice(0, source.shape[1])
        copy = pltpu.make_async_copy(source, whole.at[target, taken], sems.at[n])
        copy.start()
        started.append(copy)
    return started


def packed(entries):
    parts = []
    places = []
    for array, _, _, _ in entries:
        known = [n for n, p in enumerate(parts) if p is array]
        if not known:
            parts.append(array)
            known = [len(parts) - 1]
        places.append(known[0])
    wide = entries[0][3].stop - entries[0][3].start
    total_rows = sum(e[2] for e in entries)

    def body(offset_ref, *refs):
        ins, out, sems = refs[: len(parts)], refs[-2], refs[-1]
        started, at = [], 0
        for n, (_, _, rows, columns) in enumerate(entries):
            base = pl.multiple_of(offset_ref[n], 16)
            copy = pltpu.make_async_copy(
                ins[places[n]].at[pl.ds(base, rows), columns],
                out.at[at : at + rows, :],
                sems.at[n],
            )
            copy.start()
            started.append(copy)
            at += rows
        wait_all(started)

    return pl.pallas_call(
        body,
        grid_spec=pltpu.PrefetchScalarGridSpec(
            num_scalar_prefetch=1,
            grid=(),
            in_specs=[HBM] * len(parts),
            out_specs=VMEM,
            scratch_shapes=[pltpu.SemaphoreType.DMA((len(entries),))],
        ),
        out_shape=jax.ShapeDtypeStruct((total_rows, wide), BF16),
        cost_estimate=SLIGHT,
        compiler_params=pltpu.CompilerParams(vmem_limit_bytes=60 << 20),
    )(jnp.stack([e[1] for e in entries]).astype(jnp.int32), *parts)


def wait_all(copies):
    for copy in copies:
        copy.wait()


def by_columns(count, body):
    def step(j, carry):
        body(pl.ds(pl.multiple_of(j * WIDE, WIDE), WIDE))
        return carry

    lax.fori_loop(0, count // WIDE, step, 0)


def shapes_of(*pairs):
    return [jax.ShapeDtypeStruct(shape, dtype) for shape, dtype in pairs]


def scan_forward(rate_ref, k_ref, v_ref, since_ref, a_ref, b_ref, end_ref, cols):
    rows, wide = k_ref.shape[0], cols.stop - cols.start
    place = lax.broadcasted_iota(jnp.int32, (8, wide), 0)
    rate = rate_ref[:, cols]
    fades = [jnp.exp(-rate * float(d)) for d in (1, 2, 4)]
    carry_fade = jnp.exp(-rate * (place + 1).astype(F32))

    def step(i, state):
        base = pl.multiple_of(i * 16, 16)
        k = k_ref[pl.ds(base, 16), cols].astype(F32)
        v = v_ref[pl.ds(base, 16), cols].astype(F32)
        for h in range(2):
            at = pl.multiple_of(base + 8 * h, 8)
            part = slice(8 * h, 8 * h + 8)
            since = spread(since_ref[pl.ds(at, 8), :], wide)
            near = jnp.minimum(since, place)
            lift = jnp.exp(k[part])
            new = []
            for run, last, ref in zip((lift * v[part], lift), state, (a_ref, b_ref)):
                for d, fade in zip((1, 2, 4), fades):
                    run = run + jnp.where(near >= d, fade * pltpu.roll(run, d, 0), 0.0)
                run = run + jnp.where(since > place, carry_fade * last, 0.0)
                before = one_later(run, last)
                ref[pl.ds(at, 8), cols] = jnp.where(since >= 1, before, 0.0)
                new.append(run[7:8, :])
            state = tuple(new)
        return state

    zero = jnp.zeros((1, wide), F32)
    sa, sb = lax.fori_loop(0, rows // 16, step, (zero, zero))
    end_ref[0:1, cols] = sa
    end_ref[1:2, cols] = sb


def scan_backward(
    rate_ref,
    boost_ref,
    k_ref,
    v_ref,
    d_ref,
    a_in_ref,
    b_in_ref,
    until_ref,
    a_ref,
    b_ref,
    end_ref,
    cols,
):
    rows, wide = k_ref.shape[0], cols.stop - cols.start
    place = lax.broadcasted_iota(jnp.int32, (8, wide), 0)
    rate = rate_ref[:, cols]
    fades = [jnp.exp(-rate * float(d)) for d in (1, 2, 4)]
    carry_fade = jnp.exp(-rate * (8 - place).astype(F32))

    def step(j, state):
        base = pl.multiple_of((rows // 16 - 1 - j) * 16, 16)
        k = k_ref[pl.ds(base, 16), cols].astype(F32)
        v = v_ref[pl.ds(base, 16), cols].astype(F32)
        d = d_ref[pl.ds(base, 16), cols].astype(F32)
        for h in (1, 0):
            at = pl.multiple_of(base + 8 * h, 8)
            part = slice(8 * h, 8 * h + 8)
            until = spread(until_ref[pl.ds(at, 8), :], wide)
            near = jnp.minimum(until, 7 - place)
            bonus = jnp.exp(boost_ref[:, cols] + k[part])
            inverse = 1.0 / (b_in_ref[pl.ds(at, 8), cols] + bonus)
            wkv = (a_in_ref[pl.ds(at, 8), cols] + bonus * v[part]) * inverse
            first = d[part] * inverse
            new = []
            for run, last, ref in zip((first, -first * wkv), state, (a_ref, b_ref)):
                for q, fade in zip((1, 2, 4), fades):
                    run = run + jnp.where(near >= q, fade * pltpu.roll(run, 8 - q, 0), 0.0)
                run = run + jnp.where(until >= 8 - place, carry_fade * last, 0.0)
                ref[pl.ds(at, 8), cols] = jnp.where(until >= 1, one_earlier(run, last), 0.0)
                new.append(run[0:1, :])
            state = tuple(new)
        return state

    zero = jnp.zeros((1, wide), F32)
    sa, sb = lax.fori_loop(0, rows // 16, step, (zero, zero))
    end_ref[0:1, cols] = sa
    end_ref[1:2, cols] = sb


def carried(gap_ref, ends_ref, rate):
    cols = rate.shape[1]
    a = b = jnp.zeros((1, cols), F32)
    for j in range(gap_ref.shape[0]):
        weigh = jnp.exp(-rate * spread(gap_ref[j : j + 1, :], cols))
        a = a + weigh * ends_ref[j, 0:1, :]
        b = b + weigh * ends_ref[j, 1:2, :]
    return a, b


def norm_and_mix(track, prior, gain, bias, weights, since, others, turns):
    tokens, cols = track.shape
    count, more = len(weights), len(others)
    streams = [stream for _, stream in turns]
    inside = turns_in_kernel(cols, streams)

    def body(*refs):
        index_ref, track_ref, prior_ref, gain_ref, bias_ref, since_ref = refs[:6]
        mix_refs, other_refs = refs[6 : 6 + count], refs[6 + count : 6 + count + more]
        outs = refs[6 + count + more :]
        mixed, rest = outs[:count], outs[count:]
        gain, bias = gain_ref[...], bias_ref[...]

        def norm(z):
            centred, scale = normal(z)
            return centred * scale * gain + bias

        def step(i, last):
            at = pl.ds(pl.multiple_of(i * STEP, STEP), STEP)
            now = norm(track_ref[at, :].astype(F32))
            then = one_later(now, last)
            then = jnp.where(spread(since_ref[at, :], cols) == 0, 0.0, then)
            for out, mix_ref in zip(mixed, mix_refs):
                weight = mix_ref[...]
                out[at, :] = (now * weight + then * (1.0 - weight)).astype(BF16)
            return now[STEP - 1 :, :]

        lax.fori_loop(0, tokens // STEP, step, norm(prior_ref[...].astype(F32)))
        if inside:
            away, mine, whole = rest
            sources = [*other_refs, *mixed]
            for n, (which, _) in enumerate(turns):
                turn_blocks(index_ref, n, sources[which], whole, away, mine)

    low = ((tokens, cols), BF16)
    half = ((len(streams), cols // 2, tokens), BF16)
    index = jnp.stack([s.blocks for s in streams])
    out = pl.pallas_call(
        body,
        in_specs=[SMEM] + [VMEM] * (5 + count + more),
        out_specs=[VMEM] * (count + 2 * inside),
        out_shape=shapes_of(*[low] * count, *[half, half] * inside),
        scratch_shapes=[pltpu.VMEM((cols, tokens), BF16)] * inside,
        cost_estimate=SLIGHT,
        compiler_params=pltpu.CompilerParams(vmem_limit_bytes=60 << 20),
    )(index, track, prior, gain, bias, since, *weights, *others)
    if inside:
        return out[:count], out[count], out[count + 1]
    sources = [*others, *out]
    return out, *turned_outside([sources[which] for which, _ in turns], streams)


def keys_and_values(key_low, value_low, plans, rate, since):
    tokens, cols = key_low.shape
    parts, offsets, copies = listed(plans)
    most = max(len(c) for c in copies)

    def body(offset_ref, key_ref, value_ref, rate_ref, since_ref, *refs):
        ins = refs[: len(parts)]
        k_ref, v_ref, a_ref, b_ref, end_ref, w_k, w_v, sems = refs[len(parts) :]
        started = [
            copied(copies[n], ins, offset_ref, w, sems.at[n]) for n, w in enumerate((w_k, w_v))
        ]
        for n, (low, w, out) in enumerate(((key_ref, w_k, k_ref), (value_ref, w_v, v_ref))):
            wait_all(started[n])

            def one(at, low=low, w=w, out=out):
                out[:, at] = jnp.dot(low[...], w[:, at], preferred_element_type=F32).astype(BF16)

            by_columns(cols, one)
        end_ref[...] = jnp.zeros_like(end_ref)
        for first in range(0, cols, 256):
            scan_forward(
                rate_ref, k_ref, v_ref, since_ref, a_ref, b_ref, end_ref, slice(first, first + 256)
            )

    low, full = ((tokens, cols), BF16), ((tokens, cols), F32)
    return pl.pallas_call(
        body,
        grid_spec=pltpu.PrefetchScalarGridSpec(
            num_scalar_prefetch=1,
            grid=(),
            in_specs=[VMEM] * 4 + [HBM] * len(parts),
            out_specs=[VMEM] * 5,
            scratch_shapes=[
                pltpu.VMEM((cols, cols), BF16),
                pltpu.VMEM((cols, cols), BF16),
                pltpu.SemaphoreType.DMA((2, most)),
            ],
        ),
        out_shape=shapes_of(low, low, full, full, ((8, cols), F32)),
        cost_estimate=SLIGHT,
        compiler_params=pltpu.CompilerParams(vmem_limit_bytes=60 << 20),
    )(offsets, key_low, value_low, rate, since, *parts)


def attend(recept_low, k, v, part_a, part_b, ends, gap, rate, boost, since, track, plans):
    tokens, cols = recept_low.shape
    parts, offsets, copies = listed(plans)
    most = max(len(c) for c in copies)

    def body(offset_ref, *refs):
        low_ref, k_ref, v_ref, pa_ref, pb_ref, ends_ref, gap_ref = refs[:7]
        rate_ref, boost_ref, since_ref, track_ref = refs[7:11]
        ins = refs[11 : 11 + len(parts)]
        recept_ref, att_ref, resid_ref, a_ref, b_ref, last_ref, w_r, w_e, sems = refs[
            11 + len(parts) :
        ]
        started = [
            copied(copies[n], ins, offset_ref, w, sems.at[n]) for n, w in enumerate((w_r, w_e))
        ]
        rate, boost = rate_ref[...], boost_ref[...]
        enter_a, enter_b = carried(gap_ref, ends_ref, rate)
        wait_all(started[0])

        def gate(at):
            pre = jnp.dot(low_ref[...], w_r[:, at], preferred_element_type=F32)
            recept_ref[:, at] = jax.nn.sigmoid(pre)

        by_columns(cols, gate)

        def step(i, carry):
            at = pl.ds(pl.multiple_of(i * STEP, STEP), STEP)
            place = i * STEP + lax.broadcasted_iota(jnp.int32, (STEP, cols), 0)
            inside = spread(since_ref[at, :], cols) > place
            fade = jnp.where(inside, jnp.exp(-rate * place.astype(F32)), 0.0)
            a = pa_ref[at, :] + fade * enter_a
            b = pb_ref[at, :] + fade * enter_b
            a_ref[at, :] = a
            b_ref[at, :] = b
            bonus = jnp.exp(boost + k_ref[at, :].astype(F32))
            wkv = (a + bonus * v_ref[at, :].astype(F32)) / (b + bonus)
            low = wkv.astype(BF16).astype(F32)
            att_ref[at, :] = (recept_ref[at, :] * low).astype(BF16)
            return carry

        lax.fori_loop(0, tokens // STEP, step, 0)
        wait_all(started[1])

        def emit(at):
            out = jnp.dot(att_ref[...], w_e[:, at], preferred_element_type=F32)
            resid_ref[:, at] = track_ref[:, at].astype(F32) + out

        by_columns(cols, emit)
        last_ref[...] = resid_ref[tokens - 1 :, :]

    low, full = ((tokens, cols), BF16), ((tokens, cols), F32)
    return pl.pallas_call(
        body,
        grid_spec=pltpu.PrefetchScalarGridSpec(
            num_scalar_prefetch=1,
            grid=(),
            in_specs=[VMEM] * 11 + [HBM] * len(parts),
            out_specs=[VMEM] * 6,
            scratch_shapes=[
                pltpu.VMEM((cols, cols), BF16),
                pltpu.VMEM((cols, cols), BF16),
                pltpu.SemaphoreType.DMA((2, most)),
            ],
        ),
        out_shape=shapes_of(full, low, full, full, full, ((1, cols), F32)),
        cost_estimate=SLIGHT,
        compiler_params=pltpu.CompilerParams(vmem_limit_bytes=60 << 20),
    )(
        offsets,
        recept_low,
        k,
        v,
        part_a,
        part_b,
        ends,
        gap,
        rate,
        boost,
        since,
        track,
        *parts,
    )


def channel_mix(up_low, gate_low, resid, slope, up_weight, gate_weight, since, plans, stream):
    tokens, model = up_low.shape
    ff = plans[0][0].part.shape[-1]
    parts, offsets, copies = listed(plans)
    most = max(len(c) for c in copies)
    spans = 4
    span = ff // spans
    owners = stream.blocks.shape[0]
    block = ff // owners
    inside = block % 128 == 0

    def body(offset_ref, index_ref, up_ref, gate_ref, resid_ref, slope_ref, *refs):
        up_mix, gate_mix, since_ref = refs[:3]
        ins = refs[3 : 3 + len(parts)]
        outs = refs[3 + len(parts) :]
        mixed_ref, d_out_ref, squared_ref, d_pre_ref, d_up_ref, d_gate_ref, row_ref = outs[:7]
        w_up, w_down, w_gate, positive, sems = outs[-5:]
        gate_copies = copied(copies[2], ins, offset_ref, w_gate, sems.at[spans + 1])
        up_copies = [
            copied(
                copies[0], ins, offset_ref, w_up, sems.at[n], slice(n * span, (n + 1) * span)
            )
            for n in range(spans)
        ]
        down_copies = copied(copies[1], ins, offset_ref, w_down, sems.at[spans])
        wait_all(gate_copies)

        def gate_step(cols):
            gate = jnp.dot(gate_ref[...], w_gate[:, cols], preferred_element_type=F32)
            d_gate_ref[:, cols] = jax.nn.sigmoid(gate)

        by_columns(model, gate_step)

        def up_step(j, carry):
            cols = pl.ds(pl.multiple_of(j * WIDE, WIDE), WIDE)
            pre = jnp.dot(up_ref[...], w_up[:, cols], preferred_element_type=F32)
            pre = jnp.maximum(pre, 0.0)
            positive[:, cols] = pre
            squared_ref[:, cols] = (pre * pre).astype(BF16)
            return carry

        for n in range(spans):
            wait_all(up_copies[n])
            lax.fori_loop(n * span // WIDE, (n + 1) * span // WIDE, up_step, 0)
        wait_all(down_copies)

        def down_step(cols):
            values = jnp.dot(squared_ref[...], w_down[:, cols], preferred_element_type=F32)
            gating = d_gate_ref[:, cols]
            upstream = slope_ref[:, cols].astype(F32)
            mixed_ref[:, cols] = (resid_ref[:, cols] + gating * values).astype(BF16)
            d_out_ref[0, :, cols] = (upstream * gating).astype(BF16)
            d_out_ref[1, :, cols] = (upstream * values * gating * (1.0 - gating)).astype(BF16)

        by_columns(model, down_step)
        d_up_ref[...] = jnp.zeros_like(d_up_ref)

        def back_step(cols):
            d_squared = across(d_out_ref[0], w_down[cols, :])
            d_pre = (d_squared * 2.0 * positive[:, cols]).astype(BF16)
            d_pre_ref[:, cols] = d_pre
            d_up_ref[...] += across(d_pre, w_up[:, cols])

        by_columns(ff, back_step)

        def gate_back_step(cols):
            d_gate_ref[:, cols] = across(d_out_ref[1], w_gate[cols, :])

        by_columns(model, gate_back_step)
        row = (1.0 - up_mix[...]) * d_up_ref[0:1, :] + (1.0 - gate_mix[...]) * d_gate_ref[0:1, :]
        row_ref[...] = jnp.where(spread(since_ref[0:1, :], model) == 0, 0.0, row)
        if inside:
            away, mine = outs[7:9]

            def turn(r, carry):
                for out, half in ((away, 0), (mine, owners // 2)):
                    at = pl.multiple_of(index_ref[half + r] * block, block)
                    base = pl.multiple_of(r * block, block)
                    out[0, pl.ds(base, block), :] = squared_ref[:, pl.ds(at, block)].T
                return carry

            lax.fori_loop(0, owners // 2, turn, 0)

    low, full, wide = ((tokens, model), BF16), ((tokens, model), F32), ((tokens, ff), BF16)
    half = ((1, ff // 2, tokens), BF16)
    out = pl.pallas_call(
        body,
        grid_spec=pltpu.PrefetchScalarGridSpec(
            num_scalar_prefetch=2,
            grid=(),
            in_specs=[VMEM] * 7 + [HBM] * len(parts),
            out_specs=[VMEM] * (7 + 2 * inside),
            scratch_shapes=[
                pltpu.VMEM((model, ff), BF16),
                pltpu.VMEM((ff, model), BF16),
                pltpu.VMEM((model, model), BF16),
                pltpu.VMEM((tokens, ff), F32),
                pltpu.SemaphoreType.DMA((spans + 2, most)),
            ],
        ),
        out_shape=shapes_of(
            low,
            ((2, tokens, model), BF16),
            wide,
            wide,
            full,
            full,
            ((1, model), F32),
            *[half, half] * inside,
        ),
        cost_estimate=SLIGHT,
        compiler_params=pltpu.CompilerParams(vmem_limit_bytes=60 << 20),
    )(
        offsets,
        stream.blocks,
        up_low,
        gate_low,
        resid,
        slope,
        up_weight,
        gate_weight,
        since,
        *parts,
    )
    if inside:
        return out
    return [*out, *turned_outside([out[2]], [stream])]


def shift_back(z_of, d_of, returned, since_ref, prior, mixes, gain, bias, tokens, cols, put):
    count = len(mixes)

    def norm(z):
        centred, scale = normal(z)
        return centred * scale * gain + bias

    def lost(at):
        total = sum((1.0 - m) * d_of(n, at) for n, m in enumerate(mixes))
        return jnp.where(spread(since_ref[at, :], cols) == 0, 0.0, total)

    steps = tokens // STEP

    def step(i, carry):
        last, sums = carry[0], carry[1:]
        at = pl.ds(pl.multiple_of(i * STEP, STEP), STEP)
        z = z_of(at)
        now = norm(z)
        then = one_later(now, last)
        then = jnp.where(spread(since_ref[at, :], cols) == 0, 0.0, then)
        difference = now - then
        grads = [d_of(n, at) for n in range(count)]
        sums = [s + folded(difference * g) for s, g in zip(sums, grads)]
        ahead = jnp.minimum((i + 1) * STEP, tokens - STEP)
        ahead = lost(pl.ds(pl.multiple_of(ahead, STEP), STEP))[0:1, :]
        ahead = jnp.where(i == steps - 1, returned, ahead)
        d = one_earlier(lost(at), ahead) + sum(m * g for m, g in zip(mixes, grads))
        put(i, at, z, d)
        return (now[STEP - 1 :, :], *sums)

    zero = jnp.zeros((8, cols), F32)
    return lax.fori_loop(0, steps, step, (norm(prior), *[zero] * count))[1:]


def total(folded_sum):
    return jnp.sum(folded_sum, axis=0, keepdims=True)


def middle_back(
    d_up,
    d_gate,
    returned,
    resid,
    prior,
    slope,
    gain,
    bias,
    mixes,
    since,
    until,
    plan,
    recept,
    k,
    v,
    a,
    b,
    rate,
    boost,
):
    tokens, cols = resid.shape
    parts, offsets, copies = listed([plan])
    most = len(copies[0])

    def body(offset_ref, *refs):
        d_up_ref, d_gate_ref, returned_ref, resid_ref, prior_ref, slope_ref = refs[:6]
        gain_ref, bias_ref, up_mix, gate_mix, since_ref, until_ref = refs[6:12]
        recept_ref, k_ref, v_ref, a_ref, b_ref, rate_ref, boost_ref = refs[12:19]
        ins, rest = refs[19 : 19 + len(parts)], refs[19 + len(parts) :]
        d_resid_ref, d_att_ref, d_recept_ref, d_wkv_ref = rest[:4]
        next_a, next_b, end_ref, vec_ref = rest[4:8]
        d_attended, gain_sum, bias_sum, w_ref, sems = rest[8:]
        started = copied(copies[0], ins, offset_ref, w_ref, sems)
        gain, boost = gain_ref[...], boost_ref[...]
        gain_sum[...] = jnp.zeros_like(gain_sum)
        bias_sum[...] = jnp.zeros_like(bias_sum)

        def put(i, at, z, d):
            n, d_z = normal_back(z, d, gain)
            gain_sum[...] += folded(d * n)
            bias_sum[...] += folded(d)
            d_z = slope_ref[at, :].astype(F32) + d_z
            d_resid_ref[at, :] = d_z
            d_att_ref[at, :] = d_z.astype(BF16)

        sums = shift_back(
            lambda at: resid_ref[at, :],
            lambda n, at: (d_up_ref, d_gate_ref)[n][at, :],
            returned_ref[...],
            since_ref,
            prior_ref[...],
            [up_mix[...], gate_mix[...]],
            gain,
            bias_ref[...],
            tokens,
            cols,
            put,
        )
        vec_ref[...] = jnp.zeros_like(vec_ref)
        for n, part in enumerate([gain_sum[...], bias_sum[...], *sums]):
            vec_ref[n : n + 1, :] = total(part)

        wait_all(started)

        def back(at):
            d_attended[:, at] = across(d_att_ref[...], w_ref[at, :])

        by_columns(cols, back)

        def step(i, carry):
            at = pl.ds(pl.multiple_of(i * STEP, STEP), STEP)
            gate, d = recept_ref[at, :], d_attended[at, :]
            bonus = jnp.exp(boost + k_ref[at, :].astype(F32))
            wkv = (a_ref[at, :] + bonus * v_ref[at, :].astype(F32)) / (b_ref[at, :] + bonus)
            low = wkv.astype(BF16).astype(F32)
            d_wkv_ref[at, :] = (d * gate).astype(BF16)
            d_recept_ref[at, :] = (d * low * gate * (1.0 - gate)).astype(BF16)
            return carry

        lax.fori_loop(0, tokens // STEP, step, 0)
        end_ref[...] = jnp.zeros_like(end_ref)
        for first in range(0, cols, 256):
            scan_backward(
                rate_ref,
                boost_ref,
                k_ref,
                v_ref,
                d_wkv_ref,
                a_ref,
                b_ref,
                until_ref,
                next_a,
                next_b,
                end_ref,
                slice(first, first + 256),
            )

    low, full, vec = ((tokens, cols), BF16), ((tokens, cols), F32), ((8, cols), F32)
    return pl.pallas_call(
        body,
        grid_spec=pltpu.PrefetchScalarGridSpec(
            num_scalar_prefetch=1,
            grid=(),
            in_specs=[VMEM] * 19 + [HBM] * len(parts),
            out_specs=[VMEM] * 8,
            scratch_shapes=[
                pltpu.VMEM((tokens, cols), F32),
                pltpu.VMEM((8, cols), F32),
                pltpu.VMEM((8, cols), F32),
                pltpu.VMEM((cols, cols), BF16),
                pltpu.SemaphoreType.DMA((most,)),
            ],
        ),
        out_shape=shapes_of(full, low, low, low, full, full, vec, vec),
        cost_estimate=SLIGHT,
        compiler_params=pltpu.CompilerParams(vmem_limit_bytes=60 << 20),
    )(
        offsets,
        d_up,
        d_gate,
        returned,
        resid,
        prior,
        slope,
        gain,
        bias,
        *mixes,
        since,
        until,
        recept,
        k,
        v,
        a,
        b,
        rate,
        boost,
        *parts,
    )


def recurrence_back(back_a, back_b, heads, gap, k, v, a, b, d_wkv, until, rate, boost):
    tokens, cols = k.shape

    def body(*refs):
        back_a_ref, back_b_ref, heads_ref, gap_ref, k_ref, v_ref, a_ref, b_ref = refs[:8]
        d_ref, until_ref, rate_ref, boost_ref, d_two_ref, vec_ref = refs[8:]
        rate, boost = rate_ref[...], boost_ref[...]
        from_a, from_b = carried(gap_ref, heads_ref, rate)

        def step(i, carry):
            at = pl.ds(pl.multiple_of(i * STEP, STEP), STEP)
            place = i * STEP + lax.broadcasted_iota(jnp.int32, (STEP, cols), 0)
            inside = spread(until_ref[at, :], cols) > tokens
            fade = jnp.exp(-rate * (tokens - 1 - place).astype(F32))
            fade = jnp.where(inside, fade, 0.0)
            next_a = back_a_ref[at, :] + fade * from_a
            next_b = back_b_ref[at, :] + fade * from_b
            a, b = a_ref[at, :], b_ref[at, :]
            key, value = k_ref[at, :].astype(F32), v_ref[at, :].astype(F32)
            lift, bonus = jnp.exp(key), jnp.exp(boost + key)
            ratio = bonus / (b + bonus)
            wkv = (a + bonus * value) / (b + bonus)
            ratio = ratio * d_ref[at, :].astype(F32)
            gap_value = ratio * (value - wkv)
            d_key = gap_value + lift * (value * next_a + next_b)
            d_two_ref[0, at, :] = d_key.astype(BF16)
            d_two_ref[1, at, :] = (ratio + lift * next_a).astype(BF16)
            return carry[0] + folded(next_a * a + next_b * b), carry[1] + folded(gap_value)

        zero = jnp.zeros((8, cols), F32)
        decay, first = lax.fori_loop(0, tokens // STEP, step, (zero, zero))
        vec_ref[...] = jnp.zeros_like(vec_ref)
        vec_ref[0:1, :] = -rate * jnp.exp(-rate) * total(decay)
        vec_ref[1:2, :] = total(first)

    return pl.pallas_call(
        body,
        in_specs=[VMEM] * 12,
        out_specs=[VMEM] * 2,
        out_shape=shapes_of(((2, tokens, cols), BF16), ((8, cols), F32)),
        cost_estimate=SLIGHT,
        compiler_params=pltpu.CompilerParams(vmem_limit_bytes=60 << 20),
    )(back_a, back_b, heads, gap, k, v, a, b, d_wkv, until, rate, boost)


def entry_back(d_kv, d_recept, plans, track, prior, gain, bias, mixes, since):
    tokens, cols = track.shape
    parts, offsets, copies = listed(plans)
    most = max(len(c) for c in copies)

    def body(offset_ref, d_kv_ref, d_recept_ref, track_ref, prior_ref, gain_ref, bias_ref, *refs):
        mix_refs, since_ref = refs[:3], refs[3]
        ins, rest = refs[4 : 4 + len(parts)], refs[4 + len(parts) :]
        d_ref, row_ref, vec_ref = rest[:3]
        grads, weights, sems = rest[3:6], rest[6:9], rest[9]
        started = [
            copied(copies[n], ins, offset_ref, w, sems.at[n]) for n, w in enumerate(weights)
        ]
        lows = (d_kv_ref.at[0], d_kv_ref.at[1], d_recept_ref)
        for copies_of, low, weight, out in zip(started, lows, weights, grads):
            wait_all(copies_of)

            def one(at, low=low, weight=weight, out=out):
                out[:, at] = across(low[...], weight[at, :])

            by_columns(cols, one)

        mixes = [m[...] for m in mix_refs]

        def put(i, at, z, d):
            d_ref[at, :] = d

        sums = shift_back(
            lambda at: track_ref[at, :].astype(F32),
            lambda n, at: grads[n][at, :],
            jnp.zeros((1, cols), F32),
            since_ref,
            prior_ref[...].astype(F32),
            mixes,
            gain_ref[...],
            bias_ref[...],
            tokens,
            cols,
            put,
        )
        row = sum((1.0 - m) * g[0:1, :] for m, g in zip(mixes, grads))
        row_ref[...] = jnp.where(spread(since_ref[0:1, :], cols) == 0, 0.0, row)
        vec_ref[...] = jnp.zeros_like(vec_ref)
        for n, part in enumerate(sums):
            vec_ref[n : n + 1, :] = total(part)

    full = ((tokens, cols), F32)
    return pl.pallas_call(
        body,
        grid_spec=pltpu.PrefetchScalarGridSpec(
            num_scalar_prefetch=1,
            grid=(),
            in_specs=[VMEM] * 10 + [HBM] * len(parts),
            out_specs=[VMEM] * 3,
            scratch_shapes=[pltpu.VMEM((tokens, cols), F32)] * 3
            + [pltpu.VMEM((cols, cols), BF16)] * 3
            + [pltpu.SemaphoreType.DMA((3, most))],
        ),
        out_shape=shapes_of(full, ((1, cols), F32), ((8, cols), F32)),
        cost_estimate=SLIGHT,
        compiler_params=pltpu.CompilerParams(vmem_limit_bytes=60 << 20),
    )(offsets, d_kv, d_recept, track, prior, gain, bias, *mixes, since, *parts)


def first_norm_back(d_normed, returned, track, d_resid, gain):
    tokens, cols = track.shape

    def body(d_ref, returned_ref, track_ref, d_resid_ref, gain_ref, out_ref, vec_ref):
        gain = gain_ref[...]

        def step(i, carry):
            at = pl.ds(pl.multiple_of(i * STEP, STEP), STEP)
            place = i * STEP + lax.broadcasted_iota(jnp.int32, (STEP, cols), 0)
            d = d_ref[at, :] + jnp.where(place == tokens - 1, returned_ref[...], 0.0)
            n, d_z = normal_back(track_ref[at, :].astype(F32), d, gain)
            out_ref[at, :] = (d_resid_ref[at, :] + d_z).astype(BF16)
            return carry[0] + folded(d * n), carry[1] + folded(d)

        zero = jnp.zeros((8, cols), F32)
        gain_sum, bias_sum = lax.fori_loop(0, tokens // STEP, step, (zero, zero))
        vec_ref[...] = jnp.zeros_like(vec_ref)
        vec_ref[0:1, :] = total(gain_sum)
        vec_ref[1:2, :] = total(bias_sum)

    return pl.pallas_call(
        body,
        in_specs=[VMEM] * 5,
        out_specs=[VMEM] * 2,
        out_shape=shapes_of(((tokens, cols), BF16), ((8, cols), F32)),
        cost_estimate=SLIGHT,
        compiler_params=pltpu.CompilerParams(vmem_limit_bytes=60 << 20),
    )(d_normed, returned, track, d_resid, gain)


class Line:
    def __init__(self):
        self.last = None

    def hold(self, value):
        return value if self.last is None else after(value, self.last)

    def mark(self, value):
        self.last = value
        return value

    def pass_on(self, value):
        return self.mark(self.hold(value))


class Stream:
    def __init__(self, names):
        seq_bits = lax.axis_size("seq").bit_length() - 1
        fsdp_bits = lax.axis_size("fsdp").bit_length() - 1
        links = {"c": ("fsdp", 0), "x": ("fsdp", 1), "y": ("seq", 0)}
        links.update({f"z{i}": ("seq", i + 1) for i in range(seq_bits - 1)})
        for i in range(seq_bits - 1):
            if f"z{i}" not in names:
                names = [*names, f"z{i}"]
        self.links = [links[name] for name in names]
        places = [bit + (fsdp_bits if axis == "seq" else 0) for axis, bit in self.links]
        count = len(places)
        owners = 1 << count
        self.masks = [
            sum((1 - ((r >> (count - 1 - p)) & 1)) << place for p, place in enumerate(places))
            for r in range(owners)
        ]
        me = lax.axis_index("seq") * lax.axis_size("fsdp") + lax.axis_index("fsdp")
        self.blocks = jnp.array(self.masks, jnp.int32) ^ me.astype(jnp.int32)


def products(pairs, columns=None):
    pairs = [[x if isinstance(x, tuple) else (x, None) for x in p] for p in pairs]
    rows, tokens = pairs[0][0][0].shape[-2:]
    wide = 512
    counts = [p[2][0].shape[-1] // wide for p in pairs]
    skip = 0
    if columns is not None:
        skip, counts = columns.start // wide, [(columns.stop - columns.start) // wide]
    firsts = [sum(counts[:n]) for n in range(len(counts))]
    total = sum(counts)

    def body(*refs):
        send, keep = refs[-2:]
        for n in range(len(pairs)):
            left_a, left_b, right_a, right_b = refs[4 * n : 4 * n + 4]

            def one(left_a=left_a, left_b=left_b, right_a=right_a, right_b=right_b):
                value = jnp.dot(left_a[...], right_a[...], preferred_element_type=F32)
                value = value + jnp.dot(left_b[...], right_b[...], preferred_element_type=F32)
                send[...] = value[: rows // 2].astype(BF16)
                keep[...] = value[rows // 2 :].astype(BF16)

            if len(pairs) == 1:
                one()
            else:
                i = pl.program_id(0)
                pl.when((i >= firsts[n]) & (i < firsts[n] + counts[n]))(one)

    def spec(lead, block, index):
        if lead is None:
            return pl.BlockSpec(block, index)
        return pl.BlockSpec((None, *block), lambda i: (lead, *index(i)))

    specs = []
    for n, p in enumerate(pairs):
        for q, (_, lead) in enumerate(p):
            if q < 2:
                specs.append(spec(lead, (rows, tokens), lambda i: (0, 0)))
            else:
                specs.append(
                    spec(
                        lead,
                        (tokens, wide),
                        lambda i, n=n: (0, skip + jnp.clip(i - firsts[n], 0, counts[n] - 1)),
                    )
                )
    out = pl.BlockSpec((rows // 2, wide), lambda i: (0, i))
    shape = jax.ShapeDtypeStruct((rows // 2, total * wide), BF16)
    return pl.pallas_call(
        body,
        grid=(total,),
        in_specs=specs,
        out_specs=[out, out],
        out_shape=[shape, shape],
        cost_estimate=SLIGHT,
        compiler_params=pltpu.CompilerParams(vmem_limit_bytes=60 << 20),
    )(*[x for p in pairs for x, _ in p])


class Sum:
    def __init__(self, line, stream, pairs, columns=None):
        self.line, self.links = line, list(stream.links[1:])
        held = pairs[0][2]
        held = (line.hold(held[0]), held[1]) if isinstance(held, tuple) else line.hold(held)
        pairs[0] = (*pairs[0][:2], held, pairs[0][3])
        send, keep = products(pairs, columns)
        line.mark(send)
        self.parts = [keep]
        self.got = flipped(send, *self.links.pop(0))

    def take(self):
        self.got = self.line.pass_on(self.got)

    def step(self):
        self.parts.append(self.line.hold(self.got))
        half = self.parts[0].shape[0] // 2
        if self.links:
            send = sum(p[:half].astype(F32) for p in self.parts).astype(BF16)
            self.line.mark(send)
            self.got = flipped(send, *self.links.pop(0))
            self.parts = [p[half:] for p in self.parts]

    def total(self):
        self.parts.append(self.line.hold(self.got))
        return sum(p.astype(F32) for p in self.parts)


def on_device(
    incoming_symbols,
    downstream_slope,
    sequence_extents,
    mixer_lookup_map,
    mixer_payload_map,
    mixer_accepting_map,
    mixer_emitted_map,
    feedforward_lookup_map,
    feedforward_payload_map,
    feedforward_accepting_map,
    prime_normalize_gain,
    prime_normalize_bias,
    later_normalize_gain,
    later_normalize_bias,
    mixer_lookup_shiftmix,
    mixer_payload_shiftmix,
    mixer_accepting_shiftmix,
    feedforward_lookup_shiftmix,
    feedforward_accepting_shiftmix,
    channel_shrink_rate,
    newest_boost,
):
    track, slope = incoming_symbols[0], downstream_slope[0]
    tokens, model = track.shape
    seq_count, fsdp_count = lax.axis_size("seq"), lax.axis_size("fsdp")
    seq_number, fsdp_number = lax.axis_index("seq"), lax.axis_index("fsdp")
    here = {
        "z0": seq_number // 2 % 2,
        "y": seq_number % 2,
        "x": fsdp_number // 2,
        "c": fsdp_number % 2,
    }
    gain_one, bias_one, gain_two, bias_two, mix_key, mix_value, mix_recept, mix_up, mix_gate = [
        v[None, :]
        for v in (
            prime_normalize_gain,
            prime_normalize_bias,
            later_normalize_gain,
            later_normalize_bias,
            mixer_lookup_shiftmix,
            mixer_payload_shiftmix,
            mixer_accepting_shiftmix,
            feedforward_lookup_shiftmix,
            feedforward_accepting_shiftmix,
        )
    ]
    boost = newest_boost[None, :]
    line = Line()
    by_x = Stream(["c", "x", "y", "z0"])
    by_yx = Stream(["c", "y", "x", "z0"])
    by_zy = Stream(["c", "z0", "y", "x"])
    by_p = Stream(["c", "z0", "y", "x"])
    by_q = Stream(["c", "x", "y", "z0"])

    rows = mixer_lookup_map.shape[0]
    down_rows = feedforward_payload_map.shape[0]
    down_half = down_rows // 2
    pairs = [[i, i + 1] for i in range(0, fsdp_count, 2)]

    def by_chip(weight):
        return lax.all_gather(weight, "fsdp", axis=0, tiled=True, axis_index_groups=pairs)

    accepting_chip, emitted_chip, gate_chip, up_chip, down_chip = [
        by_chip(w)
        for w in (
            mixer_accepting_map,
            mixer_emitted_map,
            feedforward_accepting_map,
            feedforward_lookup_map,
            feedforward_payload_map,
        )
    ]

    def shard_rows(shard, size=rows):
        return (fsdp_number ^ shard) * size

    def chip_rows(size=rows):
        return here["x"] * 2 * size

    half, part = rows // 2, rows // 4
    near_y, far_y = here["y"] * half, (1 - here["y"]) * half
    quarters = [
        (b * 2 + a) * part
        for b in (here["y"], 1 - here["y"])
        for a in (here["z0"], 1 - here["z0"])
    ]
    near_z, far_z = here["z0"] * down_half, (1 - here["z0"]) * down_half
    every = slice(0, model)
    ff = feedforward_lookup_map.shape[1]
    blocks = [slice(n, n + model) for n in range(0, ff, model)]

    own = (mixer_lookup_map, mixer_payload_map)
    away_mix = line.mark(packed([(w, near_y, half, every) for w in own]))
    got_mix = flipped(away_mix, *LINKS["x"])
    away_more = packed(
        [
            (w, near_y, half, every)
            for w in line.hold(
                (mixer_accepting_map, mixer_emitted_map, feedforward_accepting_map)
            )
        ]
        + [(feedforward_lookup_map, quarters[0], part, b) for b in blocks]
    )
    got_more = flipped(line.mark(away_more), *LINKS["x"])
    prior_track = passed_along(line.hold(track[-1:]), "seq", 1)
    cores = [flipped(w, *LINKS["c"]) for w in line.hold(own)]

    group_positions = jnp.arange(tokens * seq_count, dtype=jnp.int32)
    group_flags = token_starts(line.hold(sequence_extents)[0], group_positions)
    chunk_flags = group_flags.reshape(seq_count, tokens)
    local_flags = lax.dynamic_index_in_dim(chunk_flags, seq_number, 0, keepdims=False)
    chunk_has = jnp.any(chunk_flags, axis=1)
    chunk_first = chunk_flags[:, 0]
    places = jnp.arange(tokens, dtype=jnp.int32)
    later = places[None, :] > places[:, None]
    marked = local_flags[None, :]
    last_start = jnp.max(jnp.where(marked & ~later, places[None, :], -FAR), axis=1)
    next_start = jnp.min(jnp.where(marked & later, places[None, :], FAR), axis=1)
    since = jnp.broadcast_to((places - last_start)[:, None], (tokens, 128))
    until = jnp.broadcast_to((next_start - 1 - places)[:, None], (tokens, 128))
    order = jnp.arange(seq_count, dtype=jnp.int32)
    between = (order[None, :] > order[:, None]) & (order[None, :] < seq_number)
    reaches = (order < seq_number) & ~jnp.any(between & chunk_has[None, :], axis=1)
    gap = jnp.where(reaches, ((seq_number - 1 - order) * tokens).astype(F32), NEVER)
    gap = jnp.broadcast_to(gap[:, None], (seq_count, 128))
    above = order[None, :] > seq_number
    blocked = chunk_first[None, :] & (order[None, :] <= order[:, None])
    blocked = blocked | (chunk_has[None, :] & (order[None, :] < order[:, None]))
    comes = (order > seq_number) & ~jnp.any(blocked & above, axis=1)
    gap_back = jnp.where(comes, ((order - 1 - seq_number) * tokens).astype(F32), NEVER)
    gap_back = jnp.broadcast_to(gap_back[:, None], (seq_count, 128))
    rate = jnp.exp(channel_shrink_rate)[None, :]
    line.mark((since, until, gap, gap_back, rate))

    away_down = line.mark(
        packed([(line.hold(feedforward_payload_map), near_z, down_half, every)])
    )

    got_mix = line.pass_on(got_mix)
    other_mix = flipped(got_mix, *LINKS["y"])
    (key_low, value_low, recept_low), mixer_away, mixer_mine = norm_and_mix(
        track,
        line.hold(prior_track),
        gain_one,
        bias_one,
        (mix_key, mix_value, mix_recept),
        since,
        [],
        [(0, by_q), (1, by_q), (2, by_p)],
    )
    line.mark(key_low)
    cores = line.pass_on(cores)
    other_mix = line.pass_on(other_mix)
    cross_mix = flipped(line.hold(got_mix), *LINKS["c"])
    cross_other_mix = flipped(other_mix, *LINKS["c"])

    def halves(parts, w, size, near, far):
        window = slice(w * size, (w + 1) * size)
        return [
            Piece(p, shard_rows(2 + n // 2, 2 * size) + (near, far)[n % 2], (), window)
            for n, p in enumerate(parts)
        ]

    plans_kv = [
        [
            Piece(own[w], shard_rows(0)),
            Piece(cores[w], shard_rows(1)),
            *halves((got_mix, other_mix, cross_mix, cross_other_mix), w, half, near_y, far_y),
        ]
        for w in range(2)
    ]
    k, v, part_a, part_b, ends = keys_and_values(
        line.hold(key_low), value_low, plans_kv, rate, since
    )
    line.mark(ends)
    all_ends = gathered_ends(ends[:2])
    mixer_other = flipped(line.hold(mixer_away), *LINKS["c"])
    got_down = flipped(away_down, *LINKS["x"])
    got_more = line.pass_on(got_more)
    got_rest = line.mark(got_more[: 3 * half])
    other_rest = flipped(got_rest, *LINKS["y"])
    got_up = line.mark(line.hold(got_more)[3 * half :])
    next_up = flipped(got_up, *LINKS["z0"])
    all_ends = line.pass_on(all_ends)
    mixer_other = line.pass_on(mixer_other)
    pair_up = line.mark(jnp.stack([got_up, line.hold(next_up)]))
    far_up = flipped(pair_up, *LINKS["y"])
    got_down = line.pass_on(got_down)
    other_down = flipped(got_down, *LINKS["z0"])
    other_rest = line.pass_on(other_rest)
    cross_rest = flipped(line.hold(got_rest), *LINKS["c"])
    cross_other_rest = flipped(other_rest, *LINKS["c"])
    plan_r, plan_e, plan_gate = [
        [
            Piece(chip, chip_rows()),
            *halves((got_rest, other_rest, cross_rest, cross_other_rest), w, half, near_y, far_y),
        ]
        for w, chip in enumerate((accepting_chip, emitted_chip, gate_chip))
    ]
    recept, attended, resid, state_a, state_b, last_row = attend(
        line.hold(recept_low),
        k,
        v,
        part_a,
        part_b,
        all_ends,
        gap,
        rate,
        boost,
        since,
        track,
        [plan_r, plan_e],
    )

    prior_resid = passed_along(line.mark(last_row), "seq", 1)
    prior_resid = line.hold(prior_resid)
    (up_low, gate_low), channel_away, channel_mine = norm_and_mix(
        resid,
        prior_resid,
        gain_two,
        bias_two,
        (mix_up, mix_gate),
        since,
        [attended],
        [(0, by_p), (2, by_p), (1, by_yx), (1, by_zy)],
    )
    line.mark(channel_away)
    far_up = line.pass_on(far_up)
    cross_up = flipped(line.hold(pair_up), *LINKS["c"])
    cross_far_up = flipped(far_up, *LINKS["c"])
    cross_down = flipped(line.hold(got_down), *LINKS["c"])
    other_down = line.pass_on(other_down)
    cross_other_down = flipped(other_down, *LINKS["c"])
    plan_up = [Piece(up_chip, chip_rows())]
    for shard, first, pair in ((2, 0, pair_up), (2, 2, far_up), (3, 0, cross_up), (3, 2, cross_far_up)):
        for n in range(2):
            for q, block in enumerate(blocks):
                plan_up.append(
                    Piece(
                        pair,
                        shard_rows(shard) + quarters[first + n],
                        (n,),
                        slice(q * part, (q + 1) * part),
                        block.start,
                    )
                )
    plan_down = [
        Piece(down_chip, chip_rows(down_rows)),
        *halves(
            (got_down, other_down, cross_down, cross_other_down), 0, down_half, near_z, far_z
        ),
    ]
    mixed, d_out, _, d_pre_up, d_up_in, d_gate_in, d_row, squared_away, squared_mine = (
        channel_mix(
            *line.hold((up_low, gate_low)),
            resid,
            slope,
            mix_up,
            mix_gate,
            since,
            [plan_up, plan_down, plan_gate],
            by_x,
        )
    )
    returned = passed_along(line.mark(d_row), "seq", -1)
    squared_other = flipped(squared_away, *LINKS["c"])
    d_out_other = flipped(d_out, *LINKS["c"])
    squared_other, d_out_other, returned = line.pass_on((squared_other, d_out_other, returned))
    channel_other = flipped(line.hold(channel_away), *LINKS["c"])
    d_pre_up_other = flipped(line.hold(d_pre_up), *LINKS["c"])
    sum_down = Sum(
        line, by_x, [((squared_mine, 0), (squared_other, 0), (d_out, 0), (d_out_other, 0))]
    )
    half_ff = ff // 2
    sum_up = [
        Sum(
            line,
            stream,
            [((channel_mine, 2 + n), (channel_other, 2 + n), d_pre_up, d_pre_up_other)],
            slice(n * half_ff, (n + 1) * half_ff),
        )
        for n, stream in enumerate((by_yx, by_zy))
    ]

    d_resid, d_att, d_recept, d_wkv, back_a, back_b, heads, vec_two = middle_back(
        line.hold(d_up_in),
        d_gate_in,
        returned,
        resid,
        prior_resid,
        slope,
        gain_two,
        bias_two,
        (mix_up, mix_gate),
        since,
        until,
        plan_e,
        recept,
        k,
        v,
        state_a,
        state_b,
        rate,
        boost,
    )
    line.mark(heads)
    all_heads = gathered_ends(heads[:2])
    d_att_other = flipped(d_att, *LINKS["c"])
    d_recept_other = flipped(d_recept, *LINKS["c"])
    sum_p = Sum(
        line,
        by_p,
        [
            ((channel_mine, 1), (channel_other, 1), (d_out, 1), (d_out_other, 1)),
            ((channel_mine, 0), (channel_other, 0), d_att, d_att_other),
            ((mixer_mine, 2), (mixer_other, 2), d_recept, d_recept_other),
        ],
    )
    sum_up[0].take()
    sum_up[1].take()
    d_kv, vec_state = recurrence_back(
        back_a,
        back_b,
        line.hold(all_heads),
        gap_back,
        k,
        v,
        state_a,
        state_b,
        d_wkv,
        until,
        rate,
        boost,
    )
    line.mark(vec_state)
    d_kv_other = flipped(d_kv, "fsdp", 0)
    d_normed, d_first_row, vec_one = entry_back(
        line.hold(d_kv),
        d_recept,
        [*plans_kv, plan_r],
        track,
        prior_track,
        gain_one,
        bias_one,
        (mix_key, mix_value, mix_recept),
        since,
    )
    returned_first = passed_along(line.mark(d_first_row), "seq", -1)
    sum_up[0].step()
    sum_down.step()
    sum_q = Sum(
        line,
        by_q,
        [
            ((mixer_mine, n), (mixer_other, n), (d_kv, n), (d_kv_other, n))
            for n in range(2)
        ],
    )
    sum_up[1].step()
    sum_up[0].step()
    sum_p.step()
    tokens_grad, vec_first = first_norm_back(
        d_normed, line.hold(returned_first), track, d_resid, gain_one
    )
    line.mark(vec_first)

    small = jnp.concatenate(
        [vec_first[:2], vec_two[:2], vec_one[:3], vec_two[2:4], vec_state[:2]], axis=0
    )
    owners = seq_count * fsdp_count
    share = model // owners
    small = small.reshape(-1, owners, share).transpose(1, 0, 2).reshape(owners, -1)
    line.mark(small)
    small = lax.all_to_all(small, BOTH, split_axis=0, concat_axis=0, tiled=True)
    sum_down.step()
    sum_up[1].step()
    sum_q.step()
    sum_up[0].step()
    sum_p.step()
    sum_down.step()
    sum_q.step()
    sum_up[1].step()
    sum_p.step()
    sum_q.step()
    sums = [sum_p, sum_down, *sum_up, sum_q]
    while any(s.links for s in sums):
        for s in sums:
            if s.links:
                s.step()
    grad_up = jnp.concatenate([s.total() for s in sum_up], axis=1)
    grad_down = sum_down.total()
    grad_gate, grad_output, grad_recept = jnp.split(sum_p.total(), 3, axis=1)
    grad_key, grad_value = jnp.split(sum_q.total(), 2, axis=1)
    small = jnp.sum(line.hold(small), axis=0).reshape(-1, share)
    large = (grad_key, grad_value, grad_recept, grad_output, grad_up, grad_down, grad_gate)
    return (mixed[None], tokens_grad[None], *large, *[small[i] for i in range(11)])


def solution(mesh):
    rows = P("fsdp", None)
    tokens = P("fsdp", "seq", None)
    return jax.shard_map(
        on_device,
        mesh=mesh,
        in_specs=(tokens, tokens, *[rows] * 8, *[P()] * 11),
        out_specs=(tokens, tokens, *[P(BOTH, None)] * 7, *[P(BOTH)] * 11),
        check_vma=False,
    )
```

```python
from functools import partial

import jax
import jax.numpy as jnp
from jax import lax
from jax.experimental import pallas as pl
from jax.experimental.pallas import tpu as pltpu
from jax.sharding import PartitionSpec as P

norm_eps = 1e-05
F32 = jnp.float32
BF16 = jnp.bfloat16
FAR = 1 << 20
SLIGHT = pl.CostEstimate(flops=1, bytes_accessed=1, transcendentals=0)
NEVER = 1e30
BOTH = ("seq", "fsdp")
LINKS = {"c": ("fsdp", 0), "x": ("fsdp", 1), "y": ("seq", 0), "z0": ("seq", 1)}
VMEM = pl.BlockSpec(memory_space=pltpu.VMEM)
SMEM = pl.BlockSpec(memory_space=pltpu.SMEM)
HBM = pl.BlockSpec(memory_space=pl.ANY)
WIDE = 512
STEP = 64


def after(value, *others):
    return lax.optimization_barrier((value, others))[0]


def flipped(value, axis, bit):
    count = lax.axis_size(axis)
    return lax.ppermute(value, axis, [(i, i ^ (1 << bit)) for i in range(count)])


def passed_along(value, axis, steps):
    count = lax.axis_size(axis)
    initial, last = (max(0, -steps), min(count, count - steps))
    return lax.ppermute(value, axis, [(source, source + steps) for source in range(initial, last)])


def token_starts(sequence_extents, positions):
    begins = jnp.cumsum(sequence_extents, axis=-1) - sequence_extents
    start_marks = (begins[..., :, None] == positions) & (sequence_extents[..., :, None] > 0)
    return jnp.any(start_marks, axis=-2)


def gathered_ends(copies):
    return lax.all_to_all(copies, "seq", split_axis=0, concat_axis=0, tiled=True)


def across(left, right):
    return lax.dot_general(left, right, (((1,), (1,)), ((), ())), preferred_element_type=F32)


def spread(mark, cols):
    return jnp.tile(mark, (1, cols // 128))


def normal(z):
    centred = z - jnp.mean(z, axis=-1, keepdims=True)
    return centred, lax.rsqrt(jnp.mean(centred * centred, axis=-1, keepdims=True) + norm_eps)


def normal_back(z, d, gain):
    centred, scale = normal(z)
    n = centred * scale
    e = d * gain
    inner = e - jnp.mean(e, axis=-1, keepdims=True) - n * jnp.mean(e * n, axis=-1, keepdims=True)
    return n, scale * inner


def one_later(block, previous):
    place = lax.broadcasted_iota(jnp.int32, block.shape, 0)
    return jnp.where(place == 0, previous, pltpu.roll(block, 1, 0))


def one_earlier(block, following):
    rows = block.shape[0]
    place = lax.broadcasted_iota(jnp.int32, block.shape, 0)
    return jnp.where(place == rows - 1, following, pltpu.roll(block, rows - 1, 0))


def folded(block):
    return sum(block[n : n + 8] for n in range(0, block.shape[0], 8))


def turn_blocks(stream, n, source, whole, away, mine):
    order = stream.order()
    owners = len(order)
    block = source.shape[1] // owners
    whole[...] = source[...].T
    for r in range(owners):
        base = pl.multiple_of(order[r] * block, block)
        out, at = (away, r) if r < owners // 2 else (mine, r - owners // 2)
        out[n, at * block : (at + 1) * block, :] = whole[pl.ds(base, block), :]


def turns_in_kernel(rows, streams):
    return (rows // len(streams[0].masks)) % 16 == 0


def turned_outside(acts, streams):
    rows = acts[0].shape[1]
    out = []
    for act, stream in zip(acts, streams):
        block = rows // len(stream.masks)
        blocks = jnp.stack(stream.order())
        index = blocks[:, None] * block + jnp.arange(block)[None, :]
        out.append(jnp.take(act.T, index.reshape(-1), axis=0))
    out = jnp.stack(out)
    return out[:, : rows // 2], out[:, rows // 2 :]


class Piece:
    def __init__(self, part, offset, lead=(), rows=None, column=None):
        self.part, self.offset, self.lead = part, offset, lead
        self.rows, self.column = rows, column


def listed(plans):
    parts, copies = [], []
    for plan in plans:
        copies.append([])
        for piece in plan:
            known = [n for n, p in enumerate(parts) if p is piece.part]
            if not known:
                parts.append(piece.part)
                known = [len(parts) - 1]
            copies[-1].append((known[0], piece))
    return parts, copies


def copied(copies, ins, whole, sems, columns=None):
    started = []
    for n, (part, piece) in enumerate(copies):
        source = ins[part].at[piece.lead] if piece.lead else ins[part]
        if piece.rows is not None:
            source = source.at[piece.rows, :]
        base = pl.multiple_of(piece.offset(), 16)
        target = pl.ds(base, source.shape[0])
        if piece.column is not None:
            taken = slice(piece.column, piece.column + source.shape[1])
            if columns is not None and taken.start != columns.start:
                continue
        elif columns is not None:
            taken = columns
            source = source.at[:, columns]
        else:
            taken = slice(0, source.shape[1])
        copy = pltpu.make_async_copy(source, whole.at[target, taken], sems.at[n])
        copy.start()
        started.append(copy)
    return started


def packed(entries):
    parts, places = [], []
    for array, _, _, _ in entries:
        known = [n for n, p in enumerate(parts) if p is array]
        if not known:
            parts.append(array)
            known = [len(parts) - 1]
        places.append(known[0])
    wide = entries[0][3].stop - entries[0][3].start
    total_rows = sum(e[2] for e in entries)

    def body(*refs):
        ins, out, sems = refs[: len(parts)], refs[-2], refs[-1]
        started, at = [], 0
        for n, (_, offset, rows, columns) in enumerate(entries):
            copy = pltpu.make_async_copy(
                ins[places[n]].at[pl.ds(pl.multiple_of(offset(), 16), rows), columns],
                out.at[at : at + rows, :],
                sems.at[n],
            )
            copy.start()
            started.append(copy)
            at += rows
        wait_all(started)

    return pl.pallas_call(
        body,
        in_specs=[HBM] * len(parts),
        out_specs=VMEM,
        scratch_shapes=[pltpu.SemaphoreType.DMA((len(entries),))],
        out_shape=jax.ShapeDtypeStruct((total_rows, wide), BF16),
        cost_estimate=SLIGHT,
        compiler_params=pltpu.CompilerParams(vmem_limit_bytes=60 << 20),
    )(*parts)


def wait_all(copies):
    for copy in copies:
        copy.wait()


def by_columns(count, body, wide=WIDE):
    def step(j, carry):
        body(pl.ds(pl.multiple_of(j * wide, wide), wide))
        return carry

    lax.fori_loop(0, count // wide, step, 0)


class Late:
    def __init__(self, source, ref, sem):
        self.copy, self.ref, self.waited = pltpu.make_async_copy(source, ref, sem), ref, False

    def get(self):
        if not self.waited:
            self.copy.wait()
            self.waited = True
        return self.ref


class Early:
    def __init__(self, ref, out, sem):
        self.copy, self.ref, self.sent = pltpu.make_async_copy(ref, out, sem), ref, False

    def send(self):
        self.copy.start()
        self.sent = True


def streamed(body, scalars, ins, outs, scratch=()):
    lates = [a for a, how in ins if how == "late"]
    earlies = [o for o in outs if o[2] == "early"]

    def wrapped(*refs):
        refs = list(refs)

        def pop(count):
            taken, refs[:] = refs[:count], refs[count:]
            return taken

        scalar_refs, in_refs, out_refs = pop(len(scalars)), pop(len(ins)), pop(len(outs))
        late_refs, early_refs = pop(len(lates)), pop(len(earlies))
        late_sems, early_sems = pop(1)[0], pop(1)[0]
        given, made, n = [], [], 0
        for (_, how), ref in zip(ins, in_refs):
            if how == "late":
                given.append(Late(ref, late_refs[n], late_sems.at[n]))
                n += 1
            else:
                given.append(ref)
        n = 0
        for (_, _, how), ref in zip(outs, out_refs):
            if how == "early":
                made.append(Early(early_refs[n], ref, early_sems.at[n]))
                n += 1
            else:
                made.append(ref)
        body(scalar_refs, given, made, *refs)
        for out in made:
            if isinstance(out, Early):
                if not out.sent:
                    out.send()
        for out in made:
            if isinstance(out, Early):
                out.copy.wait()

    return pl.pallas_call(
        wrapped,
        grid_spec=pltpu.PrefetchScalarGridSpec(
            num_scalar_prefetch=len(scalars),
            grid=(),
            in_specs=[VMEM if how == "now" else HBM for _, how in ins],
            out_specs=[VMEM if how == "now" else HBM for _, _, how in outs],
            scratch_shapes=[pltpu.VMEM(a.shape, a.dtype) for a in lates]
            + [pltpu.VMEM(shape, dtype) for shape, dtype, _ in earlies]
            + [
                pltpu.SemaphoreType.DMA((max(1, len(lates)),)),
                pltpu.SemaphoreType.DMA((max(1, len(earlies)),)),
            ]
            + list(scratch),
        ),
        out_shape=[jax.ShapeDtypeStruct(shape, dtype) for shape, dtype, _ in outs],
        cost_estimate=SLIGHT,
        compiler_params=pltpu.CompilerParams(vmem_limit_bytes=60 << 20),
    )(*scalars, *[a for a, _ in ins])


def start_copies(copies):
    for copy in copies:
        copy.start()


def start_all(*lates):
    for late in lates:
        late.copy.start()


def shapes_of(*pairs):
    return [jax.ShapeDtypeStruct(shape, dtype) for shape, dtype in pairs]


def scan_forward(rate_ref, k_ref, v_ref, since_ref, a_ref, b_ref, end_ref, cols):
    rows, wide = k_ref.shape[0], cols.stop - cols.start
    place = lax.broadcasted_iota(jnp.int32, (8, wide), 0)
    rate = rate_ref[:, cols]
    fades = [jnp.exp(-rate * float(d)) for d in (1, 2, 4)]
    carry_fade = jnp.exp(-rate * (place + 1).astype(F32))

    def step(i, state):
        base = pl.multiple_of(i * 16, 16)
        k = k_ref[pl.ds(base, 16), cols].astype(F32)
        v = v_ref[pl.ds(base, 16), cols].astype(F32)
        for h in range(2):
            at = pl.multiple_of(base + 8 * h, 8)
            part = slice(8 * h, 8 * h + 8)
            since = spread(since_ref[pl.ds(at, 8), :], wide)
            near = jnp.minimum(since, place)
            lift = jnp.exp(k[part])
            new = []
            for run, last, ref in zip((lift * v[part], lift), state, (a_ref, b_ref)):
                for d, fade in zip((1, 2, 4), fades):
                    run = run + jnp.where(near >= d, fade * pltpu.roll(run, d, 0), 0.0)
                run = run + jnp.where(since > place, carry_fade * last, 0.0)
                before = one_later(run, last)
                ref[pl.ds(at, 8), cols] = jnp.where(since >= 1, before, 0.0)
                new.append(run[7:8, :])
            state = tuple(new)
        return state

    zero = jnp.zeros((1, wide), F32)
    sa, sb = lax.fori_loop(0, rows // 16, step, (zero, zero))
    for n in range(end_ref.shape[0]):
        end_ref[n, 0:1, cols] = sa
        end_ref[n, 1:2, cols] = sb


def scan_backward(
    rate_ref,
    boost_ref,
    k_ref,
    v_ref,
    d_ref,
    a_in_ref,
    b_in_ref,
    until_ref,
    a_ref,
    b_ref,
    end_ref,
    cols,
):
    rows, wide = k_ref.shape[0], cols.stop - cols.start
    place = lax.broadcasted_iota(jnp.int32, (8, wide), 0)
    rate = rate_ref[:, cols]
    fades = [jnp.exp(-rate * float(d)) for d in (1, 2, 4)]
    carry_fade = jnp.exp(-rate * (8 - place).astype(F32))

    def step(j, state):
        base = pl.multiple_of((rows // 16 - 1 - j) * 16, 16)
        k = k_ref[pl.ds(base, 16), cols].astype(F32)
        v = v_ref[pl.ds(base, 16), cols].astype(F32)
        d = d_ref[pl.ds(base, 16), cols].astype(F32)
        for h in (1, 0):
            at = pl.multiple_of(base + 8 * h, 8)
            part = slice(8 * h, 8 * h + 8)
            until = spread(until_ref[pl.ds(at, 8), :], wide)
            near = jnp.minimum(until, 7 - place)
            bonus = jnp.exp(boost_ref[:, cols] + k[part])
            inverse = 1.0 / (b_in_ref[pl.ds(at, 8), cols] + bonus)
            wkv = (a_in_ref[pl.ds(at, 8), cols] + bonus * v[part]) * inverse
            first = d[part] * inverse
            new = []
            for run, last, ref in zip((first, -first * wkv), state, (a_ref, b_ref)):
                for q, fade in zip((1, 2, 4), fades):
                    run = run + jnp.where(near >= q, fade * pltpu.roll(run, 8 - q, 0), 0.0)
                run = run + jnp.where(until >= 8 - place, carry_fade * last, 0.0)
                ref[pl.ds(at, 8), cols] = jnp.where(until >= 1, one_earlier(run, last), 0.0)
                new.append(run[0:1, :])
            state = tuple(new)
        return state

    zero = jnp.zeros((1, wide), F32)
    sa, sb = lax.fori_loop(0, rows // 16, step, (zero, zero))
    for n in range(end_ref.shape[0]):
        end_ref[n, 0:1, cols] = sa
        end_ref[n, 1:2, cols] = sb


def carried(gap_ref, ends_ref, rate):
    cols = rate.shape[1]
    a = b = jnp.zeros((1, cols), F32)
    for j in range(gap_ref.shape[0]):
        weigh = jnp.exp(-rate * spread(gap_ref[j : j + 1, :], cols))
        a = a + weigh * ends_ref[j, 0:1, :]
        b = b + weigh * ends_ref[j, 1:2, :]
    return a, b


def norm_and_mix(track, prior, gain, bias, weights, since, others, turns):
    tokens, cols = track.shape
    count, more = len(weights), len(others)
    streams = [stream for _, stream in turns]
    inside = bool(turns) and turns_in_kernel(cols, streams)

    def body(*refs):
        track_ref, prior_ref, gain_ref, bias_ref, since_ref = refs[:5]
        mix_refs, other_refs = refs[5 : 5 + count], refs[5 + count : 5 + count + more]
        outs = refs[5 + count + more :]
        mixed, rest = outs[:count], outs[count:]
        gain, bias = gain_ref[...], bias_ref[...]

        def norm(z):
            centred, scale = normal(z)
            return centred * scale * gain + bias

        def step(i, last):
            at = pl.ds(pl.multiple_of(i * STEP, STEP), STEP)
            now = norm(track_ref[at, :].astype(F32))
            then = one_later(now, last)
            then = jnp.where(spread(since_ref[at, :], cols) == 0, 0.0, then)
            for out, mix_ref in zip(mixed, mix_refs):
                weight = mix_ref[...]
                out[at, :] = (now * weight + then * (1.0 - weight)).astype(BF16)
            return now[STEP - 1 :, :]

        lax.fori_loop(0, tokens // STEP, step, norm(prior_ref[...].astype(F32)))
        if inside:
            away, mine, whole = rest
            sources = [*other_refs, *mixed]
            for n, (which, _) in enumerate(turns):
                turn_blocks(streams[n], n, sources[which], whole, away, mine)

    low = ((tokens, cols), BF16)
    half = ((len(streams), cols // 2, tokens), BF16)
    out = pl.pallas_call(
        body,
        in_specs=[VMEM] * (5 + count + more),
        out_specs=[VMEM] * (count + 2 * inside),
        out_shape=shapes_of(*[low] * count, *[half, half] * inside),
        scratch_shapes=[pltpu.VMEM((cols, tokens), BF16)] * inside,
        cost_estimate=SLIGHT,
        compiler_params=pltpu.CompilerParams(vmem_limit_bytes=60 << 20),
    )(track, prior, gain, bias, since, *weights, *others)
    if inside:
        return out[:count], out[count], out[count + 1]
    if not turns:
        return out
    sources = [*others, *out]
    return out, *turned_outside([sources[which] for which, _ in turns], streams)


def keys_and_values(key_low, value_low, plans, rate, since):
    tokens, cols = key_low.shape
    parts, copies = listed(plans)
    most = max(len(c) for c in copies)

    def body(scalars, ins, outs, w_k, w_v, sems):
        key_ref, value, rate_ref, since_ref = ins[:4]
        k, v, a, b, end_ref = outs
        started = [
            copied(copies[n], ins[4:], w, sems.at[n])
            for n, w in enumerate((w_k, w_v))
        ]
        start_all(value)
        for n, (low, w, out) in enumerate(((key_ref, w_k, k), (value, w_v, v))):
            wait_all(started[n])
            low = low.get() if n else low

            def one(at, low=low, w=w, out=out):
                value = jnp.dot(low[...], w[:, at], preferred_element_type=F32)
                out.ref[:, at] = value.astype(BF16)

            by_columns(cols, one)
            out.send()
        scan_forward(
            rate_ref, k.ref, v.ref, since_ref, a.ref, b.ref, end_ref, slice(0, cols)
        )

    low, full = ((tokens, cols), BF16, "early"), ((tokens, cols), F32, "early")
    return streamed(
        body,
        [],
        [(key_low, "now"), (value_low, "late"), (rate, "now"), (since, "now")]
        + [(p, "raw") for p in parts],
        [low, low, full, full, ((lax.axis_size("seq"), 2, cols), F32, "now")],
        [
            pltpu.VMEM((cols, cols), BF16),
            pltpu.VMEM((cols, cols), BF16),
            pltpu.SemaphoreType.DMA((2, most)),
        ],
    )


def attend(recept_low, k, v, part_a, part_b, ends, gap, rate, boost, since, track, plans):
    tokens, cols = recept_low.shape
    parts, copies = listed(plans)
    most = max(len(c) for c in copies)

    def body(scalars, ins, outs, w_r, w_e, sems):
        low_ref, k, v, part_a, part_b, ends_ref, gap_ref = ins[:7]
        rate_ref, boost_ref, since_ref, track = ins[7:11]
        recept, att, resid, a_out, b_out, last_ref = outs
        started = [copied(copies[0], ins[11:], w_r, sems.at[0])]
        start_all(k, v, part_a, part_b)
        started.append(copied(copies[1], ins[11:], w_e, sems.at[1]))
        start_all(track)
        rate, boost = rate_ref[...], boost_ref[...]
        enter_a, enter_b = carried(gap_ref, ends_ref, rate)
        wait_all(started[0])

        def gate(at):
            pre = jnp.dot(low_ref[...], w_r[:, at], preferred_element_type=F32)
            recept.ref[:, at] = jax.nn.sigmoid(pre)

        by_columns(cols, gate)
        recept.send()
        k_ref, v_ref, pa_ref, pb_ref = k.get(), v.get(), part_a.get(), part_b.get()

        def step(i, carry):
            at = pl.ds(pl.multiple_of(i * STEP, STEP), STEP)
            place = i * STEP + lax.broadcasted_iota(jnp.int32, (STEP, cols), 0)
            inside = spread(since_ref[at, :], cols) > place
            fade = jnp.where(inside, jnp.exp(-rate * place.astype(F32)), 0.0)
            a = pa_ref[at, :] + fade * enter_a
            b = pb_ref[at, :] + fade * enter_b
            a_out.ref[at, :] = a
            b_out.ref[at, :] = b
            bonus = jnp.exp(boost + k_ref[at, :].astype(F32))
            wkv = (a + bonus * v_ref[at, :].astype(F32)) / (b + bonus)
            low = wkv.astype(BF16).astype(F32)
            att.ref[at, :] = (recept.ref[at, :] * low).astype(BF16)
            return carry

        lax.fori_loop(0, tokens // STEP, step, 0)
        a_out.send()
        b_out.send()
        att.send()
        wait_all(started[1])
        track_ref = track.get()

        def emit(at):
            out = jnp.dot(att.ref[...], w_e[:, at], preferred_element_type=F32)
            resid.ref[:, at] = track_ref[:, at].astype(F32) + out

        by_columns(cols, emit)
        resid.send()
        last_ref[...] = resid.ref[tokens - 1 :, :]

    low, full = ((tokens, cols), BF16, "early"), ((tokens, cols), F32, "early")
    return streamed(
        body,
        [],
        [
            (recept_low, "now"),
            (k, "late"),
            (v, "late"),
            (part_a, "late"),
            (part_b, "late"),
            (ends, "now"),
            (gap, "now"),
            (rate, "now"),
            (boost, "now"),
            (since, "now"),
            (track, "late"),
        ]
        + [(p, "raw") for p in parts],
        [full, low, full, full, full, ((1, cols), F32, "now")],
        [
            pltpu.VMEM((cols, cols), BF16),
            pltpu.VMEM((cols, cols), BF16),
            pltpu.SemaphoreType.DMA((2, most)),
        ],
    )


def channel_mix(up_low, gate_low, resid, slope, up_weight, gate_weight, since, plans, stream):
    tokens, model = up_low.shape
    ff = plans[0][0].part.shape[-1]
    parts, copies = listed(plans)
    most = max(len(c) for c in copies)
    spans = 4
    span = ff // spans
    owners = len(stream.masks)
    block = ff // owners
    inside = block % 128 == 0

    def body(scalars, ins, outs, w_up, w_down, w_gate, positive, d_up, gating, *rest):
        order = stream.order()
        up_ref, gate_ref, resid, slope, up_mix, gate_mix, since_ref = ins[:7]
        mixed, d_out, d_pre, d_up_out, d_gate, row_ref = outs[:6]
        squared, sems = rest if inside else (outs[6].ref, rest[0])
        gate_copies = copied(copies[2], ins[7:], w_gate, sems.at[spans + 1])
        up_copies = [
            copied(
                copies[0], ins[7:], w_up, sems.at[n], slice(n * span, (n + 1) * span)
            )
            for n in range(spans)
        ]
        down_copies = copied(copies[1], ins[7:], w_down, sems.at[spans])
        start_all(resid, slope)
        wait_all(gate_copies)

        def gate_step(cols):
            gate = jnp.dot(gate_ref[...], w_gate[:, cols], preferred_element_type=F32)
            gating[:, cols] = jax.nn.sigmoid(gate)

        by_columns(model, gate_step)

        def up_step(j, carry):
            cols = pl.ds(pl.multiple_of(j * WIDE, WIDE), WIDE)
            pre = jnp.dot(up_ref[...], w_up[:, cols], preferred_element_type=F32)
            pre = jnp.maximum(pre, 0.0)
            positive[:, cols] = pre
            squared[:, cols] = (pre * pre).astype(BF16)
            return carry

        for n in range(spans):
            wait_all(up_copies[n])
            lax.fori_loop(n * span // WIDE, (n + 1) * span // WIDE, up_step, 0)
        if inside:
            away, mine = outs[6:8]

            for r in range(owners):
                out, base = (away, r) if r < owners // 2 else (mine, r - owners // 2)
                at = pl.multiple_of(order[r] * block, block)
                out.ref[0, base * block : (base + 1) * block, :] = squared[:, pl.ds(at, block)].T
            away.send()
            mine.send()
        wait_all(down_copies)
        resid_ref, slope_ref = resid.get(), slope.get()

        def down_step(cols):
            values = jnp.dot(squared[...], w_down[:, cols], preferred_element_type=F32)
            gate = gating[:, cols]
            upstream = slope_ref[:, cols].astype(F32)
            mixed.ref[:, cols] = (resid_ref[:, cols] + gate * values).astype(BF16)
            d_out.ref[0, :, cols] = (upstream * gate).astype(BF16)
            d_out.ref[1, :, cols] = (upstream * values * gate * (1.0 - gate)).astype(BF16)

        by_columns(model, down_step)
        d_out.send()
        mixed.send()

        def gate_back_step(cols):
            gating[:, cols] = across(d_out.ref[1], w_gate[cols, :])

        by_columns(model, gate_back_step)
        d_gate.ref[...] = gating[...].astype(BF16)
        d_gate.send()

        def back_step(cols):
            d_squared = across(d_out.ref[0], w_down[cols, :])
            value = (d_squared * 2.0 * positive[:, cols]).astype(BF16)
            d_pre.ref[:, cols] = value
            d_up[...] += across(value, w_up[:, cols])

        d_up[...] = jnp.zeros_like(d_up)
        by_columns(ff, back_step, 1024)
        d_pre.send()
        d_up_out.ref[...] = d_up[...].astype(BF16)
        d_up_out.send()
        row = (1.0 - up_mix[...]) * d_up[0:1, :] + (1.0 - gate_mix[...]) * gating[0:1, :]
        row_ref[...] = jnp.where(spread(since_ref[0:1, :], model) == 0, 0.0, row)

    low = ((tokens, model), BF16, "early")
    half = ((1, ff // 2, tokens), BF16, "early")
    wide = ((tokens, ff), BF16, "early")
    out = streamed(
        body,
        [],
        [
            (up_low, "now"),
            (gate_low, "now"),
            (resid, "late"),
            (slope, "late"),
            (up_weight, "now"),
            (gate_weight, "now"),
            (since, "now"),
        ]
        + [(p, "raw") for p in parts],
        [
            low,
            ((2, tokens, model), BF16, "early"),
            wide,
            low,
            low,
            ((1, model), F32, "now"),
            *([half, half] if inside else [wide]),
        ],
        [
            pltpu.VMEM((model, ff), BF16),
            pltpu.VMEM((ff, model), BF16),
            pltpu.VMEM((model, model), BF16),
            pltpu.VMEM((tokens, ff), F32),
            pltpu.VMEM((tokens, model), F32),
            pltpu.VMEM((tokens, model), F32),
            *[pltpu.VMEM((tokens, ff), BF16)] * inside,
            pltpu.SemaphoreType.DMA((spans + 2, most)),
        ],
    )
    if inside:
        return out
    return [*out[:6], *turned_outside([out[6]], [stream])]


def shift_back(z_of, d_of, returned, since_ref, prior, mixes, gain, bias, tokens, cols, put):
    count = len(mixes)

    def norm(z):
        centred, scale = normal(z)
        return centred * scale * gain + bias

    gone = [1.0 - m for m in mixes]

    def lost(at, rows):
        total = sum(g * d_of(n, at)[rows] for n, g in enumerate(gone))
        return jnp.where(spread(since_ref[at, :][rows], cols) == 0, 0.0, total)

    steps = tokens // STEP

    def step(i, carry):
        last, sums = carry[0], carry[1:]
        at = pl.ds(pl.multiple_of(i * STEP, STEP), STEP)
        z = z_of(at)
        now = norm(z)
        then = one_later(now, last)
        then = jnp.where(spread(since_ref[at, :], cols) == 0, 0.0, then)
        difference = now - then
        grads = [d_of(n, at) for n in range(count)]
        sums = [s + folded(difference * g) for s, g in zip(sums, grads)]
        ahead = jnp.minimum((i + 1) * STEP, tokens - STEP)
        ahead = lost(pl.ds(pl.multiple_of(ahead, STEP), 16), slice(0, 1))
        ahead = jnp.where(i == steps - 1, returned, ahead)
        d = one_earlier(lost(at, slice(None)), ahead) + sum(m * g for m, g in zip(mixes, grads))
        put(i, at, z, d)
        return (now[STEP - 1 :, :], *sums)

    zero = jnp.zeros((8, cols), F32)
    return lax.fori_loop(0, steps, step, (norm(prior), *[zero] * count))[1:]


def total(folded_sum):
    return jnp.sum(folded_sum, axis=0, keepdims=True)


def middle_back(
    d_up,
    d_gate,
    returned,
    resid,
    prior,
    slope,
    gain,
    bias,
    mixes,
    since,
    until,
    plan,
    recept,
    k,
    v,
    a,
    b,
    rate,
    boost,
):
    tokens, cols = resid.shape
    parts, copies = listed([plan])
    most = len(copies[0])

    def body(scalars, ins, outs, d_attended, gain_sum, bias_sum, w_ref, sems):
        d_up_ref, d_gate_ref, returned_ref, resid_ref, prior_ref, slope_ref = ins[:6]
        gain_ref, bias_ref, up_mix, gate_mix, since_ref, until_ref = ins[6:12]
        recept, k, v, a, b, rate_ref, boost_ref = ins[12:19]
        d_resid, d_att, d_recept, d_wkv, next_a, next_b, end_ref, vec_ref = outs
        started = copied(copies[0], ins[19:], w_ref, sems)
        start_all(recept, k, v, a, b)
        gain, boost = gain_ref[...], boost_ref[...]
        gain_sum[...] = jnp.zeros_like(gain_sum)
        bias_sum[...] = jnp.zeros_like(bias_sum)

        def put(i, at, z, d):
            n, d_z = normal_back(z, d, gain)
            gain_sum[...] += folded(d * n)
            bias_sum[...] += folded(d)
            d_z = slope_ref[at, :].astype(F32) + d_z
            d_resid.ref[at, :] = d_z
            d_att.ref[at, :] = d_z.astype(BF16)

        sums = shift_back(
            lambda at: resid_ref[at, :],
            lambda n, at: (d_up_ref, d_gate_ref)[n][at, :].astype(F32),
            returned_ref[...],
            since_ref,
            prior_ref[...],
            [up_mix[...], gate_mix[...]],
            gain,
            bias_ref[...],
            tokens,
            cols,
            put,
        )
        d_att.send()
        d_resid.send()
        vec_ref[...] = jnp.zeros_like(vec_ref)
        for n, part in enumerate([gain_sum[...], bias_sum[...], *sums]):
            vec_ref[n : n + 1, :] = total(part)
        wait_all(started)

        def back(at):
            d_attended[:, at] = across(d_att.ref[...], w_ref[at, :])

        by_columns(cols, back)
        recept_ref, k_ref, v_ref, a_ref, b_ref = [x.get() for x in (recept, k, v, a, b)]

        def step(i, carry):
            at = pl.ds(pl.multiple_of(i * STEP, STEP), STEP)
            gate, d = recept_ref[at, :], d_attended[at, :]
            bonus = jnp.exp(boost + k_ref[at, :].astype(F32))
            wkv = (a_ref[at, :] + bonus * v_ref[at, :].astype(F32)) / (b_ref[at, :] + bonus)
            low = wkv.astype(BF16).astype(F32)
            d_wkv.ref[at, :] = (d * gate).astype(BF16)
            d_recept.ref[at, :] = (d * low * gate * (1.0 - gate)).astype(BF16)
            return carry

        lax.fori_loop(0, tokens // STEP, step, 0)
        d_recept.send()
        d_wkv.send()
        scan_backward(
            rate_ref,
            boost_ref,
            k_ref,
            v_ref,
            d_wkv.ref,
            a_ref,
            b_ref,
            until_ref,
            next_a.ref,
            next_b.ref,
            end_ref,
            slice(0, cols),
        )

    low, full = ((tokens, cols), BF16, "early"), ((tokens, cols), F32, "early")
    vec = ((8, cols), F32, "now")
    return streamed(
        body,
        [],
        [
            (x, "now")
            for x in (d_up, d_gate, returned, resid, prior, slope, gain, bias, *mixes, since, until)
        ]
        + [(x, "late") for x in (recept, k, v, a, b)]
        + [(rate, "now"), (boost, "now")]
        + [(p, "raw") for p in parts],
        [
            full,
            low,
            low,
            low,
            full,
            full,
            ((lax.axis_size("seq"), 2, cols), F32, "now"),
            vec,
        ],
        [
            pltpu.VMEM((tokens, cols), F32),
            pltpu.VMEM((8, cols), F32),
            pltpu.VMEM((8, cols), F32),
            pltpu.VMEM((cols, cols), BF16),
            pltpu.SemaphoreType.DMA((most,)),
        ],
    )


def recurrence_back(back_a, back_b, heads, gap, k, v, a, b, d_wkv, until, rate, boost):
    tokens, cols = k.shape

    def body(*refs):
        back_a_ref, back_b_ref, heads_ref, gap_ref, k_ref, v_ref, a_ref, b_ref = refs[:8]
        d_ref, until_ref, rate_ref, boost_ref, d_key_ref, d_value_ref, vec_ref = refs[8:]
        rate, boost = rate_ref[...], boost_ref[...]
        from_a, from_b = carried(gap_ref, heads_ref, rate)

        def step(i, carry):
            at = pl.ds(pl.multiple_of(i * STEP, STEP), STEP)
            place = i * STEP + lax.broadcasted_iota(jnp.int32, (STEP, cols), 0)
            inside = spread(until_ref[at, :], cols) > tokens
            fade = jnp.exp(-rate * (tokens - 1 - place).astype(F32))
            fade = jnp.where(inside, fade, 0.0)
            next_a = back_a_ref[at, :] + fade * from_a
            next_b = back_b_ref[at, :] + fade * from_b
            a, b = a_ref[at, :], b_ref[at, :]
            key, value = k_ref[at, :].astype(F32), v_ref[at, :].astype(F32)
            lift, bonus = jnp.exp(key), jnp.exp(boost + key)
            ratio = bonus / (b + bonus)
            wkv = (a + bonus * value) / (b + bonus)
            ratio = ratio * d_ref[at, :].astype(F32)
            gap_value = ratio * (value - wkv)
            d_key = gap_value + lift * (value * next_a + next_b)
            d_key_ref[at, :] = d_key.astype(BF16)
            d_value_ref[at, :] = (ratio + lift * next_a).astype(BF16)
            return carry[0] + folded(next_a * a + next_b * b), carry[1] + folded(gap_value)

        zero = jnp.zeros((8, cols), F32)
        decay, first = lax.fori_loop(0, tokens // STEP, step, (zero, zero))
        vec_ref[...] = jnp.zeros_like(vec_ref)
        vec_ref[0:1, :] = -rate * jnp.exp(-rate) * total(decay)
        vec_ref[1:2, :] = total(first)

    return pl.pallas_call(
        body,
        in_specs=[VMEM] * 12,
        out_specs=[VMEM] * 3,
        out_shape=shapes_of(((tokens, cols), BF16), ((tokens, cols), BF16), ((8, cols), F32)),
        cost_estimate=SLIGHT,
        compiler_params=pltpu.CompilerParams(vmem_limit_bytes=60 << 20),
    )(back_a, back_b, heads, gap, k, v, a, b, d_wkv, until, rate, boost)


def entry_back(d_key, d_value, d_recept, plans, track, prior, gain, bias, mixes, since):
    tokens, cols = track.shape
    parts, copies = listed(plans)
    most = max(len(c) for c in copies)

    def body(*refs):
        lows, (track_ref, prior_ref, gain_ref, bias_ref) = refs[:3], refs[3:7]
        mix_refs, since_ref = refs[7:10], refs[10]
        ins, rest = refs[11 : 11 + len(parts)], refs[11 + len(parts) :]
        d_ref, row_ref, vec_ref = rest[:3]
        grads, weights, sems = rest[3:6], rest[6:9], rest[9]
        started = [
            copied(copies[n], ins, w, sems.at[n]) for n, w in enumerate(weights)
        ]
        for copies_of, low, weight, out in zip(started, lows, weights, grads):
            wait_all(copies_of)

            def one(at, low=low, weight=weight, out=out):
                out[:, at] = across(low[...], weight[at, :])

            by_columns(cols, one)

        mixes = [m[...] for m in mix_refs]

        def put(i, at, z, d):
            d_ref[at, :] = d

        sums = shift_back(
            lambda at: track_ref[at, :].astype(F32),
            lambda n, at: grads[n][at, :],
            jnp.zeros((1, cols), F32),
            since_ref,
            prior_ref[...].astype(F32),
            mixes,
            gain_ref[...],
            bias_ref[...],
            tokens,
            cols,
            put,
        )
        row = sum((1.0 - m) * g[0:1, :] for m, g in zip(mixes, grads))
        row_ref[...] = jnp.where(spread(since_ref[0:1, :], cols) == 0, 0.0, row)
        vec_ref[...] = jnp.zeros_like(vec_ref)
        for n, part in enumerate(sums):
            vec_ref[n : n + 1, :] = total(part)

    full = ((tokens, cols), F32)
    return pl.pallas_call(
        body,
        in_specs=[VMEM] * 11 + [HBM] * len(parts),
        out_specs=[VMEM] * 3,
        scratch_shapes=[pltpu.VMEM((tokens, cols), F32)] * 3
        + [pltpu.VMEM((cols, cols), BF16)] * 3
        + [pltpu.SemaphoreType.DMA((3, most))],
        out_shape=shapes_of(full, ((1, cols), F32), ((8, cols), F32)),
        cost_estimate=SLIGHT,
        compiler_params=pltpu.CompilerParams(vmem_limit_bytes=60 << 20),
    )(d_key, d_value, d_recept, track, prior, gain, bias, *mixes, since, *parts)


def first_norm_back(d_normed, returned, track, d_resid, gain):
    tokens, cols = track.shape

    def body(d_ref, returned_ref, track_ref, d_resid_ref, gain_ref, out_ref, vec_ref):
        gain = gain_ref[...]

        def step(i, carry):
            at = pl.ds(pl.multiple_of(i * STEP, STEP), STEP)
            place = i * STEP + lax.broadcasted_iota(jnp.int32, (STEP, cols), 0)
            d = d_ref[at, :] + jnp.where(place == tokens - 1, returned_ref[...], 0.0)
            n, d_z = normal_back(track_ref[at, :].astype(F32), d, gain)
            out_ref[at, :] = (d_resid_ref[at, :] + d_z).astype(BF16)
            return carry[0] + folded(d * n), carry[1] + folded(d)

        zero = jnp.zeros((8, cols), F32)
        gain_sum, bias_sum = lax.fori_loop(0, tokens // STEP, step, (zero, zero))
        vec_ref[...] = jnp.zeros_like(vec_ref)
        vec_ref[0:1, :] = total(gain_sum)
        vec_ref[1:2, :] = total(bias_sum)

    return pl.pallas_call(
        body,
        in_specs=[VMEM] * 5,
        out_specs=[VMEM] * 2,
        out_shape=shapes_of(((tokens, cols), BF16), ((8, cols), F32)),
        cost_estimate=SLIGHT,
        compiler_params=pltpu.CompilerParams(vmem_limit_bytes=60 << 20),
    )(d_normed, returned, track, d_resid, gain)


class Line:
    def __init__(self):
        self.last = None

    def hold(self, value):
        return value if self.last is None else after(value, self.last)

    def mark(self, value):
        self.last = value
        return value

    def pass_on(self, value):
        return self.mark(self.hold(value))


class Stream:
    def __init__(self, names):
        seq_bits = lax.axis_size("seq").bit_length() - 1
        fsdp_bits = lax.axis_size("fsdp").bit_length() - 1
        links = {"c": ("fsdp", 0), "x": ("fsdp", 1), "y": ("seq", 0)}
        links.update({f"z{i}": ("seq", i + 1) for i in range(seq_bits - 1)})
        for i in range(seq_bits - 1):
            if f"z{i}" not in names:
                names = [*names, f"z{i}"]
        self.links = [links[name] for name in names]
        places = [bit + (fsdp_bits if axis == "seq" else 0) for axis, bit in self.links]
        count = len(places)
        owners = 1 << count
        self.masks = [
            sum((1 - ((r >> (count - 1 - p)) & 1)) << place for p, place in enumerate(places))
            for r in range(owners)
        ]
        self.fsdp_count = lax.axis_size("fsdp")

    def order(self):
        me = lax.axis_index("seq") * self.fsdp_count + lax.axis_index("fsdp")
        return [me ^ mask for mask in self.masks]


def products(pairs, columns=None):
    pairs = [[x if isinstance(x, tuple) else (x, None) for x in p] for p in pairs]
    rows, tokens = pairs[0][0][0].shape[-2:]
    apart = columns is not None
    columns = columns or [slice(0, p[2][0].shape[-1]) for p in pairs]
    span = 1024
    tasks = [
        (n, slice(c, c + span))
        for n, window in enumerate(columns)
        for c in range(window.start, window.stop, span)
    ]
    places, widths = [], [0]
    for t, (n, _) in enumerate(tasks):
        if apart and t and tasks[t - 1][0] != n:
            widths.append(0)
        places.append((len(widths) - 1, widths[-1]))
        widths[-1] += span
    arrays, numbers = [], []
    for p in pairs:
        for array, _ in p:
            known = [n for n, other in enumerate(arrays) if other is array]
            if not known:
                arrays.append(array)
                known = [len(arrays) - 1]
            numbers.append(known[0])

    def body(scalars, ins, outs, lefts, rights, left_sems, right_sems, send, keep, out_sems):
        def source(n, q):
            ref = ins[numbers[4 * n + q]]
            lead = pairs[n][q][1]
            return ref if lead is None else ref.at[lead]

        coming, loaded = [], {}
        for t, (n, cols) in enumerate(tasks):
            if n not in loaded:
                loaded[n] = [
                    pltpu.make_async_copy(source(n, q), lefts.at[n, q], left_sems.at[n, q])
                    for q in range(2)
                ]
                start_copies(loaded[n])
            coming.append(
                [
                    pltpu.make_async_copy(
                        source(n, 2 + q).at[:, cols], rights.at[t, q], right_sems.at[t, q]
                    )
                    for q in range(2)
                ]
            )
            start_copies(coming[-1])
        going, seen = [], set()
        for t, (n, _) in enumerate(tasks):
            if n not in seen:
                wait_all(loaded[n])
                seen.add(n)
            wait_all(coming[t])
            for c in range(0, span, WIDE):
                at = slice(c, c + WIDE)
                value = jnp.dot(lefts[n, 0], rights[t, 0, :, at], preferred_element_type=F32)
                value = value + jnp.dot(
                    lefts[n, 1], rights[t, 1, :, at], preferred_element_type=F32
                )
                send[t, :, at] = value[: rows // 2].astype(BF16)
                keep[t, :, at] = value[rows // 2 :].astype(BF16)
            which, first = places[t]
            out_cols = slice(first, first + span)
            for q, (ref, out) in enumerate(((send, outs[2 * which]), (keep, outs[2 * which + 1]))):
                copy = pltpu.make_async_copy(ref.at[t], out.at[:, out_cols], out_sems.at[t, q])
                copy.start()
                going.append(copy)
        wait_all(going)

    count = len(tasks)
    return streamed(
        body,
        [],
        [(a, "raw") for a in arrays],
        [((rows // 2, width), BF16, "raw") for width in widths for _ in range(2)],
        [
            pltpu.VMEM((len(pairs), 2, rows, tokens), BF16),
            pltpu.VMEM((count, 2, tokens, span), BF16),
            pltpu.SemaphoreType.DMA((len(pairs), 2)),
            pltpu.SemaphoreType.DMA((count, 2)),
            pltpu.VMEM((count, rows // 2, span), BF16),
            pltpu.VMEM((count, rows // 2, span), BF16),
            pltpu.SemaphoreType.DMA((count, 2)),
        ],
    )


def added(groups, dtype):
    out = []
    for parts, _, rows in groups:
        out.append(sum(a[first : first + rows].astype(F32) for a, first in parts).astype(dtype))
    return jnp.concatenate(out, axis=1)


def added_by_kernel(groups, dtype):
    rows = groups[0][2]
    if rows % 16:
        return added(groups, dtype)
    entries = [(a, first, g) for g, (parts, _, _) in enumerate(groups) for a, first in parts]
    widths = [cols for _, cols, _ in groups]

    def body(scalars, ins, outs, sems, *held):
        coming = []
        for n, (_, first, g) in enumerate(entries):
            coming.append(
                pltpu.make_async_copy(ins[n].at[first : first + rows, :], held[n], sems.at[n])
            )
        start_copies(coming)
        wait_all(coming)
        at = 0
        for g, width in enumerate(widths):
            mine = [held[n] for n, entry in enumerate(entries) if entry[2] == g]

            def one(i, carry, mine=mine, at=at, width=width):
                part = pl.ds(pl.multiple_of(i * 16, 16), 16)
                value = sum(ref[part, :].astype(F32) for ref in mine)
                outs[0].ref[part, at : at + width] = value.astype(dtype)
                return carry

            lax.fori_loop(0, rows // 16, one, 0)
            at += width

    return streamed(
        body,
        [],
        [(a, "raw") for a, _, _ in entries],
        [((rows, sum(widths)), dtype, "early")],
        [pltpu.SemaphoreType.DMA((len(entries),))]
        + [pltpu.VMEM((rows, widths[g]), BF16) for _, _, g in entries],
    )[0]


class Sum:
    def __init__(self, line, stream, pairs, ready=None, wait=False):
        self.line, self.links = line, list(stream.links[1:])
        if ready is None:
            held = pairs[0][2]
            held = (line.hold(held[0]), held[1]) if isinstance(held, tuple) else line.hold(held)
            pairs[0] = (*pairs[0][:2], held, pairs[0][3])
            ready = line.mark(products(pairs))
        send, keep = ready
        self.rows, self.cols = keep.shape
        self.parts = [(keep, 0)]
        self.send = send
        if not wait:
            self.go()

    def go(self):
        self.got = flipped(self.send, *self.links.pop(0))

    def take(self):
        self.got = self.line.pass_on(self.got)

    def group(self):
        self.parts.append((self.line.hold(self.got), 0))
        if not self.links:
            return self.parts, self.cols, self.rows
        self.rows //= 2
        group = (self.parts, self.cols, self.rows)
        self.parts = [(a, first + self.rows) for a, first in self.parts]
        return group

    def step(self, add=None):
        step_together([self], add or added)

    def total(self):
        group = self.group()
        return added([group], F32)


def step_together(sums, add=added):
    groups = [s.group() for s in sums]
    links = [s.links.pop(0) for s in sums]
    send = add(groups, BF16)
    sums[0].line.mark(send)
    got = flipped(send, *links[0])
    at = 0
    for s in sums:
        s.got = got if len(sums) == 1 else got[:, at : at + s.cols]
        at += s.cols


def on_device(
    incoming_symbols,
    downstream_slope,
    sequence_extents,
    mixer_lookup_map,
    mixer_payload_map,
    mixer_accepting_map,
    mixer_emitted_map,
    feedforward_lookup_map,
    feedforward_payload_map,
    feedforward_accepting_map,
    prime_normalize_gain,
    prime_normalize_bias,
    later_normalize_gain,
    later_normalize_bias,
    mixer_lookup_shiftmix,
    mixer_payload_shiftmix,
    mixer_accepting_shiftmix,
    feedforward_lookup_shiftmix,
    feedforward_accepting_shiftmix,
    channel_shrink_rate,
    newest_boost,
):
    track, slope = incoming_symbols[0], downstream_slope[0]
    tokens, model = track.shape
    seq_count, fsdp_count = lax.axis_size("seq"), lax.axis_size("fsdp")
    seq_number = lax.axis_index("seq")
    gain_one, bias_one, gain_two, bias_two, mix_key, mix_value, mix_recept, mix_up, mix_gate = [
        v[None, :]
        for v in (
            prime_normalize_gain,
            prime_normalize_bias,
            later_normalize_gain,
            later_normalize_bias,
            mixer_lookup_shiftmix,
            mixer_payload_shiftmix,
            mixer_accepting_shiftmix,
            feedforward_lookup_shiftmix,
            feedforward_accepting_shiftmix,
        )
    ]
    boost = newest_boost[None, :]
    line = Line()
    by_x = Stream(["c", "x", "z0", "y"])
    by_yx = Stream(["c", "y", "x", "z0"])
    by_zx = Stream(["c", "z0", "x", "y"])
    by_p = Stream(["c", "y", "z0", "x"])
    by_q = Stream(["c", "x", "y", "z0"])

    rows = mixer_lookup_map.shape[0]
    down_rows = feedforward_payload_map.shape[0]
    down_half = down_rows // 2
    pairs = [[i, i + 1] for i in range(0, fsdp_count, 2)]

    def by_chip(weight):
        return lax.all_gather(weight, "fsdp", axis=0, tiled=True, axis_index_groups=pairs)

    def bit(name):
        axis, number = LINKS[name]
        return (lax.axis_index(axis) >> number) & 1

    def shard_rows(shard, size=rows, shift=None):
        def offset():
            base = (lax.axis_index("fsdp") ^ shard) * size
            return base if shift is None else base + shift()

        return offset

    def chip_rows(size=rows):
        return lambda: bit("x") * 2 * size

    half, part = rows // 2, rows // 4

    def near_y():
        return bit("y") * half

    def far_y():
        return (1 - bit("y")) * half

    quarters = [
        lambda i=i, j=j: ((bit("y") ^ i) * 2 + (bit("z0") ^ j)) * part
        for i in range(2)
        for j in range(2)
    ]

    def near_z():
        return bit("z0") * down_half

    def far_z():
        return (1 - bit("z0")) * down_half

    every = slice(0, model)
    ff = feedforward_lookup_map.shape[1]
    blocks = [slice(n, n + model) for n in range(0, ff, model)]

    own = (mixer_lookup_map, mixer_payload_map)
    away_mix = line.mark(packed([(w, near_y, half, every) for w in own]))
    got_mix = flipped(away_mix, *LINKS["x"])
    (
        lookup_chip,
        payload_chip,
        accepting_chip,
        emitted_chip,
        gate_chip,
        up_chip,
        down_chip,
    ) = [
        by_chip(line.hold(w))
        for w in (
            mixer_lookup_map,
            mixer_payload_map,
            mixer_accepting_map,
            mixer_emitted_map,
            feedforward_accepting_map,
            feedforward_lookup_map,
            feedforward_payload_map,
        )
    ]

    away_more = packed(
        [
            (w, near_y, half, every)
            for w in line.hold(
                (mixer_accepting_map, mixer_emitted_map, feedforward_accepting_map)
            )
        ]
        + [(feedforward_lookup_map, quarters[0], part, b) for b in blocks]
    )
    got_more = flipped(line.mark(away_more), *LINKS["x"])
    prior_track = line.pass_on(passed_along(line.hold(track[-1:]), "seq", 1))

    group_positions = jnp.arange(tokens * seq_count, dtype=jnp.int32)
    group_flags = token_starts(line.hold(sequence_extents)[0], group_positions)
    chunk_flags = group_flags.reshape(seq_count, tokens)
    local_flags = lax.dynamic_index_in_dim(chunk_flags, seq_number, 0, keepdims=False)
    chunk_has = jnp.any(chunk_flags, axis=1)
    chunk_first = chunk_flags[:, 0]
    places = jnp.arange(tokens, dtype=jnp.int32)
    later = places[None, :] > places[:, None]
    marked = local_flags[None, :]
    last_start = jnp.max(jnp.where(marked & ~later, places[None, :], -FAR), axis=1)
    next_start = jnp.min(jnp.where(marked & later, places[None, :], FAR), axis=1)
    since = jnp.broadcast_to((places - last_start)[:, None], (tokens, 128))
    until = jnp.broadcast_to((next_start - 1 - places)[:, None], (tokens, 128))
    order = jnp.arange(seq_count, dtype=jnp.int32)
    between = (order[None, :] > order[:, None]) & (order[None, :] < seq_number)
    reaches = (order < seq_number) & ~jnp.any(between & chunk_has[None, :], axis=1)
    gap = jnp.where(reaches, ((seq_number - 1 - order) * tokens).astype(F32), NEVER)
    gap = jnp.broadcast_to(gap[:, None], (seq_count, 128))
    above = order[None, :] > seq_number
    blocked = chunk_first[None, :] & (order[None, :] <= order[:, None])
    blocked = blocked | (chunk_has[None, :] & (order[None, :] < order[:, None]))
    comes = (order > seq_number) & ~jnp.any(blocked & above, axis=1)
    gap_back = jnp.where(comes, ((order - 1 - seq_number) * tokens).astype(F32), NEVER)
    gap_back = jnp.broadcast_to(gap_back[:, None], (seq_count, 128))
    rate = jnp.exp(channel_shrink_rate)[None, :]
    line.mark((since, until, gap, gap_back, rate))

    away_down = line.mark(
        packed([(line.hold(feedforward_payload_map), near_z, down_half, every)])
    )

    got_mix = line.pass_on(got_mix)
    other_mix = flipped(got_mix, *LINKS["y"])
    key_low, value_low, recept_low = norm_and_mix(
        track,
        line.hold(prior_track),
        gain_one,
        bias_one,
        (mix_key, mix_value, mix_recept),
        since,
        [],
        [],
    )
    line.mark(key_low)
    other_mix = line.pass_on(other_mix)
    cross_mix = flipped(line.hold(got_mix), *LINKS["c"])
    cross_other_mix = flipped(other_mix, *LINKS["c"])

    def halves(parts, w, size, near, far):
        window = slice(w * size, (w + 1) * size)
        return [
            Piece(p, shard_rows(2 + n // 2, 2 * size, (near, far)[n % 2]), (), window)
            for n, p in enumerate(parts)
        ]

    plans_kv = [
        [
            Piece((lookup_chip, payload_chip)[w], chip_rows()),
            *halves((got_mix, other_mix, cross_mix, cross_other_mix), w, half, near_y, far_y),
        ]
        for w in range(2)
    ]
    got_down = flipped(away_down, *LINKS["x"])
    k, v, part_a, part_b, ends = keys_and_values(
        line.hold(key_low), value_low, plans_kv, rate, since
    )
    line.mark(ends)
    all_ends = gathered_ends(ends)
    got_more = line.pass_on(got_more)
    got_rest = line.mark(got_more[: 3 * half])
    other_rest = flipped(got_rest, *LINKS["y"])
    got_up = line.mark(line.hold(got_more)[3 * half :])
    next_up = flipped(got_up, *LINKS["z0"])
    pair_up = line.mark(jnp.stack([got_up, line.hold(next_up)]))
    far_up = flipped(pair_up, *LINKS["y"])
    all_ends = line.pass_on(all_ends)
    got_down = line.pass_on(got_down)
    other_down = flipped(got_down, *LINKS["z0"])
    other_rest = line.pass_on(other_rest)
    cross_rest = flipped(line.hold(got_rest), *LINKS["c"])
    cross_other_rest = flipped(other_rest, *LINKS["c"])
    plan_r, plan_e, plan_gate = [
        [
            Piece(chip, chip_rows()),
            *halves((got_rest, other_rest, cross_rest, cross_other_rest), w, half, near_y, far_y),
        ]
        for w, chip in enumerate((accepting_chip, emitted_chip, gate_chip))
    ]
    recept, attended, resid, state_a, state_b, last_row = attend(
        line.hold(recept_low),
        k,
        v,
        part_a,
        part_b,
        all_ends,
        gap,
        rate,
        boost,
        since,
        track,
        [plan_r, plan_e],
    )

    prior_resid = passed_along(line.mark(last_row), "seq", 1)
    prior_resid = line.hold(prior_resid)
    (up_low, gate_low), channel_away, channel_mine = norm_and_mix(
        resid,
        prior_resid,
        gain_two,
        bias_two,
        (mix_up, mix_gate),
        since,
        [attended, key_low, value_low, recept_low],
        [(0, by_p), (5, by_p), (4, by_yx), (4, by_zx), (1, by_q), (2, by_q), (3, by_p)],
    )
    line.mark(channel_away)
    cross_up = flipped(line.hold(pair_up), *LINKS["c"])
    cross_down = flipped(line.hold(got_down), *LINKS["c"])
    far_up = line.pass_on(far_up)
    cross_far_up = flipped(far_up, *LINKS["c"])
    other_down = line.pass_on(other_down)
    cross_other_down = flipped(other_down, *LINKS["c"])
    plan_up = [Piece(up_chip, chip_rows())]
    for shard, first, pair in ((2, 0, pair_up), (2, 2, far_up), (3, 0, cross_up), (3, 2, cross_far_up)):
        for n in range(2):
            for q, block in enumerate(blocks):
                plan_up.append(
                    Piece(
                        pair,
                        shard_rows(shard, shift=quarters[first + n]),
                        (n,),
                        slice(q * part, (q + 1) * part),
                        block.start,
                    )
                )
    plan_down = [
        Piece(down_chip, chip_rows(down_rows)),
        *halves(
            (got_down, other_down, cross_down, cross_other_down), 0, down_half, near_z, far_z
        ),
    ]
    mixed, d_out, d_pre_up, d_up_in, d_gate_in, d_row, squared_away, squared_mine = (
        channel_mix(
            *line.hold((up_low, gate_low)),
            resid,
            slope,
            mix_up,
            mix_gate,
            since,
            [plan_up, plan_down, plan_gate],
            by_x,
        )
    )
    returned = passed_along(line.mark(d_row), "seq", -1)
    squared_other = flipped(squared_away, *LINKS["c"])
    d_out_other = flipped(d_out, *LINKS["c"])
    squared_other, d_out_other = line.pass_on((squared_other, d_out_other))
    channel_other = flipped(line.hold(channel_away), *LINKS["c"])
    d_pre_up_other = flipped(line.hold(d_pre_up), *LINKS["c"])
    sum_down = Sum(
        line, by_x, [((squared_mine, 0), (squared_other, 0), (d_out, 0), (d_out_other, 0))]
    )
    returned = line.pass_on(returned)
    half_ff = ff // 2
    up_keep = products(
        [
            ((channel_mine, 2 + n), (channel_other, 2 + n), line.hold(d_pre_up), d_pre_up_other)
            for n in range(2)
        ],
        [slice(n * half_ff, (n + 1) * half_ff) for n in range(2)],
    )
    line.mark(up_keep)
    sum_up = [
        Sum(line, stream, None, ready=up_keep[2 * n : 2 * n + 2])
        for n, stream in enumerate((by_yx, by_zx))
    ]

    d_resid, d_att, d_recept, d_wkv, back_a, back_b, heads, vec_two = middle_back(
        line.hold(d_up_in),
        d_gate_in,
        returned,
        resid,
        prior_resid,
        slope,
        gain_two,
        bias_two,
        (mix_up, mix_gate),
        since,
        until,
        plan_e,
        recept,
        k,
        v,
        state_a,
        state_b,
        rate,
        boost,
    )
    line.mark(heads)
    all_heads = gathered_ends(heads)
    d_att_other = flipped(d_att, *LINKS["c"])
    d_recept_other = flipped(d_recept, *LINKS["c"])
    sum_p = Sum(
        line,
        by_p,
        [
            ((channel_mine, 1), (channel_other, 1), (d_out, 1), (d_out_other, 1)),
            ((channel_mine, 0), (channel_other, 0), d_att, d_att_other),
            ((channel_mine, 6), (channel_other, 6), d_recept, d_recept_other),
        ],
        wait=True,
    )
    all_heads = line.pass_on(all_heads)
    sum_p.send = line.pass_on(sum_p.send)
    sum_p.go()
    sum_up[0].take()
    sum_up[1].take()
    d_key, d_value, vec_state = recurrence_back(
        line.hold(back_a),
        back_b,
        all_heads,
        gap_back,
        k,
        v,
        state_a,
        state_b,
        d_wkv,
        until,
        rate,
        boost,
    )
    line.mark(vec_state)
    sum_down.step(added_by_kernel)
    step_together(sum_up, added_by_kernel)
    d_key_other = flipped(line.hold(d_key), *LINKS["c"])
    d_value_other = flipped(d_value, *LINKS["c"])
    d_normed, d_first_row, vec_one = entry_back(
        line.hold(d_key),
        d_value,
        d_recept,
        [*plans_kv, plan_r],
        track,
        prior_track,
        gain_one,
        bias_one,
        (mix_key, mix_value, mix_recept),
        since,
    )
    returned_first = passed_along(line.mark(d_first_row), "seq", -1)
    sum_q = Sum(
        line,
        by_q,
        [
            ((channel_mine, 4), (channel_other, 4), d_key, d_key_other),
            ((channel_mine, 5), (channel_other, 5), d_value, d_value_other),
        ],
    )
    sum_p.step(added_by_kernel)
    sum_down.step(added_by_kernel)
    returned_first = line.pass_on(returned_first)
    sum_up[1].step(added_by_kernel)
    sum_up[0].step(added_by_kernel)
    tokens_grad, vec_first = first_norm_back(
        line.hold(d_normed), returned_first, track, d_resid, gain_one
    )
    line.mark(vec_first)
    sum_q.take()
    sum_q.step(added_by_kernel)
    sum_p.step(added_by_kernel)

    small = jnp.concatenate(
        [vec_first[:2], vec_two[:2], vec_one[:3], vec_two[2:4], vec_state[:2]], axis=0
    )
    owners = seq_count * fsdp_count
    share = model // owners
    small = small.reshape(-1, owners, share).transpose(1, 0, 2).reshape(owners, -1)
    line.mark(small)
    small = lax.all_to_all(small, BOTH, split_axis=0, concat_axis=0, tiled=True)
    step_together(sum_up)
    sums = [sum_down, sum_q, sum_p, *sum_up]
    while any(s.links for s in sums):
        for s in sums:
            if s.links:
                s.step()
    grad_up = jnp.concatenate([s.total() for s in sum_up], axis=1)
    grad_down = sum_down.total()
    grad_gate, grad_output, grad_recept = jnp.split(sum_p.total(), 3, axis=1)
    grad_key, grad_value = jnp.split(sum_q.total(), 2, axis=1)
    small = jnp.sum(line.hold(small), axis=0).reshape(-1, share)
    large = (grad_key, grad_value, grad_recept, grad_output, grad_up, grad_down, grad_gate)
    return (mixed[None], tokens_grad[None], *large, *[small[i] for i in range(11)])


def solution(mesh):
    rows = P("fsdp", None)
    tokens = P("fsdp", "seq", None)
    return jax.shard_map(
        on_device,
        mesh=mesh,
        in_specs=(tokens, tokens, *[rows] * 8, *[P()] * 11),
        out_specs=(tokens, tokens, *[P(BOTH, None)] * 7, *[P(BOTH)] * 11),
        check_vma=False,
    )
```
